256 devices in a mesh: pipe: 16 (over x, y_hi, core), expert: 16 (over y_lo, z).
Axes of the slice: x: 4, y: 4 (y_hi: 2, y_lo: 2; y = y_hi * 2 + y_lo), z: 8, core: 2. Of those that a mesh axis runs over, the one named last changes fastest.
Arguments:
- tokens: bfloat16 [2048, 7168], P('expert'), may hold values from -6 to 6
- route_ids: int32 [2048, 8], P('expert'), may hold values from 0 to 255, all different within a row; in each aligned block of 128 rows (0 to 127, 128 to 255, ...) at most 8 rows name the same one
- route_gates: float32 [2048, 8], P('expert'), may hold values from 0.05 to 1
- w_gate: bfloat16 [16, 7168, 2048], P('expert', None, 'pipe'), may hold values from -0.0625 to 0.0625
- w_up: bfloat16 [16, 7168, 2048], P('expert', None, 'pipe'), may hold values from -0.0625 to 0.0625
- w_down: bfloat16 [16, 2048, 7168], P('expert', 'pipe'), may hold values from -0.125 to 0.125
- out_grad: bfloat16 [2048, 7168], P('expert'), may hold values from -6 to 6
- latent_grad: bfloat16 [16, 2048, 512], P('pipe', 'expert'), may hold values from -0.119628906 to 0.119628906
Outputs:
- routed: bfloat16 [2048, 7168], P('expert')
- token_grad: bfloat16 [2048, 7168], P('expert')
- kv_grad: bfloat16 [16, 7168, 512], P('pipe', 'expert')
The draws below stay inside these ranges and needn't reach their ends.
Inputs may be any that keep to these rules, and one draw needn't show every extreme that they name: `route_ids`: each row names 8 different experts. In the rows of one device no expert is named by more than 8 rows. Only experts below 16 are computed.
All inputs are finite; a program needn't handle non-finite values.
Results may differ from the reference program's by a relative error of at most 0.024.
Values may be sent and summed in bfloat16 or wider, within the bound.
No kernel may reach another device: no remote copies, remote signals or barrier semaphores. Data moves between devices by JAX's collectives and lax.ppermute only.
A program may use at most 192 MiB of HBM per device.

```python
import math
import jax
import jax.numpy as jnp
import numpy as np
from jax import lax

D = 7168
FF = 2048
EXPERTS_ALL = 256
TOPK = 8
KVR = 512
TOK_DEV = 128
SLOT = 8
EXPERTS = 16
TOKENS = 2048
N_PIPE = 16
N_EXPERT = 16


def raised(values, stream_key, source, target, shards_of, factor):
    def block_of(dim):
        return (jnp.arange(values.shape[dim]) // (values.shape[dim] // shards_of)).reshape((-1,) + (1,) * (values.ndim - 1 - dim))

    near = jax.random.permutation(stream_key, shards_of)[block_of(target)]
    other_side = (block_of(target) + shards_of // 2) % shards_of
    return jnp.where((block_of(source) == near) | (block_of(source) == other_side), factor * values, values)


def block_scale(rng, dims, cuts, least, high):
    level, own = 1.0, jax.random.fold_in(rng, 6)
    for position, blocks in cuts:
        steps = jnp.exp(jax.random.uniform(jax.random.fold_in(own, position), (blocks,), jnp.float32, least / len(cuts), high / len(cuts)))
        level = level * jnp.repeat(steps, dims[position] // blocks).reshape([-1 if axis == position else 1 for axis in range(len(dims))])
    return level


def assign_block(key, own, number, rows, number_of, top, bound, lean):
    sequence = jax.random.permutation(key, number_of)
    crowded, common = load_shares(number_of, rows * top, bound, lean, True), load_shares(number_of, rows * top, bound, lean, False)
    places = jnp.arange(number_of)

    def named(sizes, turn):
        used = int((sizes > 0).sum())
        fixed = max(1, used // 4)
        shifted = fixed + (places - fixed + turn * (used - fixed)) % max(1, number_of - fixed)
        return jnp.zeros((number_of,), jnp.int32).at[sequence[jnp.where(places < fixed, places, shifted)]].set(jnp.asarray(sizes, jnp.int32))

    sizes = jnp.where(number % 4 == 0, named(crowded, number // 4), named(common, number - number // 4 - 1))
    mixed = jax.random.permutation(jax.random.fold_in(own, 3), number_of)
    source_of, taker = mixed[0:number_of // 2 * 2:2], mixed[1:number_of // 2 * 2:2]
    margin = jnp.minimum(sizes[source_of] - 1, bound - sizes[taker]) // 2
    margin = jnp.where((source_of == sequence[0]) | (taker == sequence[0]) | (sizes[taker] == 0), 0, jnp.maximum(margin, 0))
    shifted = jax.random.randint(jax.random.fold_in(own, 4), (number_of // 2,), 0, 1 << 20) % (margin + 1)
    sizes = sizes.at[source_of].add(-shifted).at[taker].add(shifted)
    members = jnp.searchsorted(jnp.cumsum(sizes), jnp.arange(rows * top), side="right").astype(jnp.int32)
    grid = members.reshape(top, rows).T
    grid = grid[jax.random.permutation(jax.random.fold_in(own, 1), rows)]
    turn = jax.random.randint(jax.random.fold_in(own, 2), (rows, 1), 0, top)
    return jnp.take_along_axis(grid, (jnp.arange(top)[None, :] + turn) % top, axis=1)


def load_shares(count, total, bound, lean, full):
    weights = [(1 << 20) // math.isqrt(rank ** lean) + 1 for rank in range(1, count + 1)]
    largest = bound if full else min(bound, max(-(-total // count), total * weights[0] // sum(weights)))
    least = 1 if total - largest >= count - 1 else 0
    holding, rest = [largest] + [least] * (count - 1), total - largest - least * (count - 1)
    while rest > 0:
        free = [i for i in range(1, count) if holding[i] < largest] or [i for i in range(1, count) if holding[i] < bound]
        mass, budget = sum([weights[i] for i in free]), rest
        for i in free:
            addition = min(bound - holding[i], max(1, budget * weights[i] // mass), rest)
            holding[i] = holding[i] + addition
            rest = rest - addition
    return np.array(holding)


def gaussian(own_key, extent, width, most, pieces=(), kind=jnp.bfloat16):
    values = width * jax.random.normal(own_key, extent, jnp.float32)
    if pieces:
        values = values * block_scale(own_key, extent, pieces, -0.22, 0.18)
    return jnp.clip(values, -most, most).astype(kind)


def gaussian_with(key, extent, scale, bound, pieces, heavy, kind=jnp.bfloat16):
    values = scale * jax.random.normal(key, extent, jnp.float32)
    if pieces:
        values = values * block_scale(key, extent, pieces, -0.22, 0.18)
    return jnp.clip(raised(values, jax.random.fold_in(key, 3), *heavy), -bound, bound).astype(kind)


def setup_inputs(seed: int = 0) -> dict:
    arg_keys = jax.random.split(jax.random.key(seed), 9)
    tokens = gaussian_with(arg_keys[0], (TOKENS, D), 1.0, 6.0, ((0, 16),), (0, 1, 16, 2.0))
    route_ids_keys = jax.random.split(jax.random.fold_in(arg_keys[1], 1), TOKENS // TOK_DEV)
    route_ids_turns = jax.random.permutation(jax.random.fold_in(arg_keys[1], 3), TOKENS // TOK_DEV)
    route_ids = jax.vmap(lambda own, number: assign_block(jax.random.fold_in(arg_keys[1], 2), own, number, TOK_DEV, EXPERTS_ALL, TOPK, SLOT, 1))(route_ids_keys, route_ids_turns).reshape((TOKENS, TOPK))
    route_gates = jnp.clip(jnp.exp(math.log(1.0) - 2.9957323 * jax.random.uniform(arg_keys[2], (TOKENS, TOPK), jnp.float32) ** block_scale(arg_keys[2], (TOKENS, TOPK), ((0, 16),), -0.2, 0.2)), 0.05, 1.0)
    w_gate = gaussian(arg_keys[3], (EXPERTS, D, FF), D ** -0.5, 0.0625, ((0, 16), (2, 16)))
    w_up = gaussian(arg_keys[4], (EXPERTS, D, FF), D ** -0.5, 0.0625, ((0, 16), (2, 16)))
    w_down = gaussian(arg_keys[5], (EXPERTS, FF, D), FF ** -0.5, 0.125, ((0, 16), (1, 16)))
    out_grad = gaussian(arg_keys[6], (TOKENS, D), 1.0, 6.0, ((0, 16),))
    latent_grad = gaussian(arg_keys[7], (N_PIPE, TOKENS, KVR), 0.02, 0.119628906, ((0, 16), (1, 16)))
    return dict(tokens=tokens, route_ids=route_ids, route_gates=route_gates, w_gate=w_gate, w_up=w_up, w_down=w_down, out_grad=out_grad, latent_grad=latent_grad)


def routing(ids, gates, n_exp):
    tok = ids.shape[0]
    topk = ids.shape[1]
    flat = ids.reshape(-1)
    inside = flat < n_exp
    onehot = jnp.logical_and(flat[:, None] == jnp.arange(n_exp, dtype=jnp.int32)[None, :], inside[:, None]).astype(jnp.int32)
    before = jnp.cumsum(onehot, axis=0) - onehot
    place = jnp.sum(before * onehot, axis=1)
    target = jnp.where(inside, flat * SLOT + place, -1)
    match = (target[:, None] == jnp.arange(n_exp * SLOT, dtype=jnp.int32)[None, :]).reshape(tok, topk, n_exp * SLOT)
    match = match.astype(gates.dtype)
    select = jnp.sum(match, axis=1)
    weights = jnp.sum(match * gates[:, :, None], axis=1)
    return select, weights


def expert_forward(args):
    rows, wg, wu, wd = args
    gate_act = jnp.dot(rows, wg, preferred_element_type=jnp.float32)
    up_act = jnp.dot(rows, wu, preferred_element_type=jnp.float32)
    hidden = (jax.nn.silu(gate_act) * up_act).astype(jnp.bfloat16)
    return jnp.dot(hidden, wd, preferred_element_type=jnp.float32).astype(jnp.bfloat16)


def expert_backward(args):
    rows, drows, wg, wu, wd = args
    gate_act = jnp.dot(rows, wg, preferred_element_type=jnp.float32)
    up_act = jnp.dot(rows, wu, preferred_element_type=jnp.float32)
    hidden_grad = jnp.dot(drows, wd.T, preferred_element_type=jnp.float32)
    sg = jax.nn.sigmoid(gate_act)
    gate_grad = (hidden_grad * up_act * sg * (1.0 + gate_act * (1.0 - sg))).astype(jnp.bfloat16)
    up_grad = (hidden_grad * gate_act * sg).astype(jnp.bfloat16)
    total = jnp.dot(gate_grad, wg.T, preferred_element_type=jnp.float32) + jnp.dot(up_grad, wu.T, preferred_element_type=jnp.float32)
    return total.astype(jnp.bfloat16)


def to_owner(sent, n_exp):
    return sent.reshape(n_exp, n_exp, SLOT, D).transpose(1, 0, 2, 3).reshape(n_exp, n_exp * SLOT, D)


def reference(tokens, route_ids, route_gates, w_gate, w_up, w_down, out_grad, latent_grad):
    n_exp = N_EXPERT
    ids = route_ids.reshape(n_exp, TOK_DEV, TOPK)
    gates = route_gates.reshape(n_exp, TOK_DEV, TOPK)
    select, weights = jax.vmap(lambda i, g: routing(i, g, n_exp))(ids, gates)
    highest = lax.Precision.HIGHEST
    xs = tokens.reshape(n_exp, TOK_DEV, D).astype(jnp.float32)
    sent = jnp.einsum('stj,std->sjd', select.astype(jnp.float32), xs, precision=highest)
    rows = to_owner(sent, n_exp).astype(jnp.bfloat16)
    expert_out = lax.map(expert_forward, (rows, w_gate, w_up, w_down))
    back = to_owner(expert_out, n_exp).astype(jnp.float32)
    routed = jnp.einsum('stj,sjd->std', weights.astype(jnp.float32), back, precision=highest)
    routed = routed.astype(jnp.bfloat16).reshape(TOKENS, D)
    dys = out_grad.reshape(n_exp, TOK_DEV, D).astype(jnp.float32)
    dsent = jnp.einsum('stj,std->sjd', weights.astype(jnp.float32), dys, precision=highest).astype(jnp.bfloat16)
    drows = to_owner(dsent, n_exp)
    input_grad = lax.map(expert_backward, (rows, drows, w_gate, w_up, w_down))
    dback = to_owner(input_grad, n_exp).astype(jnp.float32)
    token_grad = jnp.einsum('stj,sjd->std', select.astype(jnp.float32), dback, precision=highest)
    token_grad = token_grad.astype(jnp.bfloat16).reshape(TOKENS, D)
    lat = latent_grad.reshape(N_PIPE, n_exp, TOK_DEV, KVR)

    def per_section(block):
        part = jnp.einsum('std,stk->sdk', xs, block.astype(jnp.float32), precision=highest)
        rounded = lax.optimization_barrier(part.astype(jnp.bfloat16))
        return jnp.sum(rounded.astype(jnp.float32), axis=0)

    section_grad = lax.map(per_section, lat)
    kv_grad = (section_grad + section_grad[::-1]).astype(jnp.bfloat16)
    return routed, token_grad, kv_grad
```

```python
import numpy as np
import jax
import jax.numpy as jnp
from jax import lax
from jax.sharding import PartitionSpec as P

SLOT = 8
BF = jnp.bfloat16
F32 = jnp.float32
CORE, Y_HI, X_LOW = 1, 2, 4


def across(value, mask):
    return lax.ppermute(value, "pipe", [(i, i ^ mask) for i in range(16)])


def delta(p, j):
    return (p & 1) * 8 + j * 4 + (p >> 2)


def shifted(value, j):
    pairs = [(p * 16 + e, p * 16 + (e ^ delta(p, j))) for p in range(16) for e in range(16)]
    return lax.ppermute(value, ("pipe", "expert"), pairs)


def gather_x(block):
    return [block] + [across(block, X_LOW * off) for off in (1, 2, 3)]


def scatter_x(partial):
    size = partial.shape[0] // 4
    total = partial[:size].astype(F32)
    parts = [across(partial[k * size : (k + 1) * size], X_LOW * k) for k in (1, 2, 3)]
    for part in parts:
        total = total + part.astype(F32)
    return total.astype(BF)


def dispatch(sent):
    block = jnp.concatenate([shifted(sent[:SLOT], 0), shifted(sent[SLOT:], 1)], axis=0)
    return jnp.concatenate(gather_x(block), axis=0)


def collect(partial):
    half = scatter_x(partial)
    full = (half.astype(F32) + across(half, Y_HI).astype(F32)).astype(BF)
    block = jnp.concatenate([shifted(full[:SLOT], 0), shifted(full[SLOT:], 1)], axis=0)
    own = jnp.concatenate(gather_x(block), axis=0)
    return jnp.concatenate([own, across(own, CORE)], axis=0)


def routing(ids, gates, experts):
    match = ids[None] == experts[:, None, None]
    named = jnp.any(match, axis=2)
    gate = jnp.sum(jnp.where(match, gates[None], 0.0), axis=2)
    tok = ids.shape[0]
    earlier = jnp.asarray(np.triu(np.ones((tok, tok), np.float32), 1), BF)
    before = jnp.dot(named.astype(BF), earlier, preferred_element_type=F32)
    slots = jnp.arange(SLOT, dtype=F32)
    sel = jnp.logical_and(named[:, None, :], before[:, None, :] == slots[None, :, None])
    mix = jnp.where(sel, gate[:, None, :], 0.0)
    rows = experts.shape[0] * SLOT
    return sel.reshape(rows, tok), mix.reshape(rows, tok)


def rdot(a, b):
    return jnp.dot(a, b, preferred_element_type=F32)


def tdot(a, b):
    return jnp.einsum("rd,fd->rf", a, b, preferred_element_type=F32)


def ldot(a, b):
    return jnp.einsum("rt,rd->td", a, b, preferred_element_type=F32)


def per_device(tokens, route_ids, route_gates, w_gate, w_up, w_down, out_grad, latent_grad):
    p = lax.axis_index("pipe")
    s = lax.axis_index("expert")
    wg, wu, wd = w_gate[0], w_up[0], w_down[0]
    wg2, wu2, wd2 = across(wg, CORE), across(wu, CORE), across(wd, CORE)

    latent = latent_grad[0]
    width = latent.shape[1] // 2
    low = p < 8
    mine = jnp.where(low, latent[:, :width], latent[:, width:])
    other = jnp.where(low, latent[:, width:], latent[:, :width])
    got = lax.ppermute(other, "pipe", [(i, 15 - i) for i in range(16)])
    both = (mine.astype(F32) + got.astype(F32)).astype(BF)
    part = jnp.einsum("td,tk->dk", tokens, both, preferred_element_type=F32).astype(BF)
    share = lax.psum_scatter(part, "expert", scatter_dimension=0, tiled=True)
    theirs = lax.ppermute(share, "pipe", [(i, 15 - i) for i in range(16)])
    kv_grad = jnp.concatenate(
        [jnp.where(low, share, theirs), jnp.where(low, theirs, share)], axis=1
    )[None]

    order = np.array([c * 8 + j * 4 + x for c in (0, 1) for x in range(4) for j in (0, 1)])
    experts = s ^ delta(p, 0) ^ jnp.asarray(order, jnp.int32)
    sel, mix = routing(route_ids, route_gates, experts)
    sel_bf = sel.astype(BF)
    first = sel_bf[: 2 * SLOT]
    sent = rdot(first, tokens).astype(BF)
    slot_gate = jnp.sum(mix[: 2 * SLOT], axis=1)
    dsent = (rdot(first, out_grad) * slot_gate[:, None]).astype(BF)

    rows = dispatch(sent)
    drows = dispatch(dsent)

    gate_act = jnp.concatenate([rdot(rows, wg), rdot(rows, wg2)], axis=1)
    up_act = jnp.concatenate([rdot(rows, wu), rdot(rows, wu2)], axis=1)
    sg = jax.nn.sigmoid(gate_act)
    hidden = (gate_act * sg * up_act).astype(BF)
    f = wg.shape[1]
    partial = (rdot(hidden[:, :f], wd) + rdot(hidden[:, f:], wd2)).astype(BF)
    back = collect(partial)
    mix_hi = mix.astype(BF)
    mix_lo = (mix - mix_hi.astype(F32)).astype(BF)
    routed = (ldot(mix_hi, back) + ldot(mix_lo, back)).astype(BF)

    hidden_grad = jnp.concatenate([tdot(drows, wd), tdot(drows, wd2)], axis=1)
    gate_grad = (hidden_grad * up_act * sg * (1.0 + gate_act * (1.0 - sg))).astype(BF)
    up_grad = (hidden_grad * gate_act * sg).astype(BF)
    dpartial = (
        tdot(gate_grad[:, :f], wg)
        + tdot(gate_grad[:, f:], wg2)
        + tdot(up_grad[:, :f], wu)
        + tdot(up_grad[:, f:], wu2)
    ).astype(BF)
    dback = collect(dpartial)
    token_grad = ldot(sel_bf, dback).astype(BF)
    return routed, token_grad, kv_grad


def solution(mesh):
    return jax.shard_map(
        per_device,
        mesh=mesh,
        in_specs=(
            P("expert", None),
            P("expert", None),
            P("expert", None),
            P("expert", None, "pipe"),
            P("expert", None, "pipe"),
            P("expert", "pipe", None),
            P("expert", None),
            P("pipe", "expert", None),
        ),
        out_specs=(P("expert", None), P("expert", None), P("pipe", "expert", None)),
        check_vma=False,
    )
```

```python
import functools
import jax
import jax.numpy as jnp
from jax import lax
from jax.experimental import pallas as pl
from jax.experimental.pallas import tpu as pltpu
from jax.sharding import PartitionSpec as P

SLOT = 8
BF = jnp.bfloat16
F32 = jnp.float32
CORE, Y_HI, X_LOW = 1, 2, 4
STEPS = 4


def across(value, mask):
    return lax.ppermute(value, "pipe", [(i, i ^ mask) for i in range(16)])


def delta(p, k):
    return (p & 1) * 8 + (k ^ ((p >> 1) & 1)) * 4 + (p >> 2)


def shifted(value, k, mask=0):
    pairs = [
        (p * 16 + e, (p ^ mask) * 16 + (e ^ delta(p, k))) for p in range(16) for e in range(16)
    ]
    return lax.ppermute(value, ("pipe", "expert"), pairs)


def along_x(value, step):
    pairs = []
    for i in range(16):
        hop = 3 if (i & 1) ^ step else 1
        pairs.append((i, i ^ (X_LOW * hop)))
    return lax.ppermute(value, "pipe", pairs)


def dispatch(first, second):
    block = jnp.concatenate([shifted(first, 0), shifted(second, 1)], axis=0)
    two = jnp.concatenate([block, along_x(block, 0)], axis=0)
    return jnp.concatenate([two, along_x(two, 1)], axis=0)


def add(a, b):
    return (a.astype(F32) + b.astype(F32)).astype(BF)


def collect(kept, sent):
    two = add(kept, along_x(sent, 1))
    size = two.shape[0] // 2
    one = add(two[:size], along_x(two[size:], 0))
    full = add(one[:SLOT], across(one[SLOT:], Y_HI))
    block = jnp.concatenate([shifted(full, 0), shifted(full, 0, Y_HI)], axis=0)
    two = jnp.concatenate([block, along_x(block, 0)], axis=0)
    far = along_x(two, 1)
    return two, far, across(two, CORE), across(far, CORE)


def dot(a, b):
    return jnp.dot(a, b, preferred_element_type=F32)


def tdot(a, b):
    return lax.dot_general(a, b, (((1,), (1,)), ((), ())), preferred_element_type=F32)


def select_kernel(
    where_ref, ids_ref, gates_ref, tok_ref, grad_ref, lat_ref,
    send0, send1, dsend0, dsend1, sel_ref, hi_ref, lo_ref, mine_ref, other_ref,
    pick, weight,
):
    @pl.when(pl.program_id(0) == 0)
    def _():
        p, s = where_ref[0], where_ref[1]
        ids, gates = ids_ref[...], gates_ref[...]
        tok = ids.shape[0]
        row = lax.broadcasted_iota(jnp.int32, (tok, tok), 0)
        lane = lax.broadcasted_iota(jnp.int32, (tok, tok), 1)
        far_core, k = lane >> 6, (lane >> 3) & 1
        ring = (lane >> 4) & 3
        off = ring ^ (ring >> 1)
        off = off ^ (2 * (off & 1) * ((p & 1) ^ far_core))
        base = s ^ ((p & 1) * 8 + ((p >> 1) & 1) * 4 + (p >> 2))
        expert = base ^ (far_core * 8) ^ (k * 4) ^ off
        named = jnp.zeros((tok, tok), F32)
        gate = jnp.zeros((tok, tok), F32)
        for choice in range(ids.shape[1]):
            hit = ids[:, choice : choice + 1] == expert
            named = jnp.where(hit, 1.0, named)
            gate = jnp.where(hit, gates[:, choice : choice + 1], gate)
        earlier = jnp.where(lane < row, 1.0, 0.0).astype(BF)
        before = dot(earlier, named.astype(BF))
        here = jnp.logical_and(named > 0.5, before == (lane & (SLOT - 1)).astype(F32))
        sel = jnp.where(here, 1.0, 0.0)
        mix = jnp.where(here, gate, 0.0)
        sel_ref[...] = sel.astype(BF)
        hi = mix.astype(BF)
        hi_ref[...] = hi
        lo_ref[...] = (mix - hi.astype(F32)).astype(BF)
        pick[...] = sel.T[: 2 * SLOT].astype(BF)
        total = jnp.sum(mix.T[: 2 * SLOT], axis=1, keepdims=True)
        weight[...] = jnp.broadcast_to(total, weight.shape)
        lat = lat_ref[0]
        width = lat.shape[1] // 2
        low = p < 8
        mine_ref[...] = jnp.where(low, lat[:, :width], lat[:, width:])
        other_ref[...] = jnp.where(low, lat[:, width:], lat[:, :width])

    rows = dot(pick[...], tok_ref[...]).astype(BF)
    drows = (dot(pick[...], grad_ref[...]) * weight[:, :1]).astype(BF)
    send0[...] = rows[:SLOT]
    send1[...] = rows[SLOT:]
    dsend0[...] = drows[:SLOT]
    dsend1[...] = drows[SLOT:]


def whole(shape):
    return pl.BlockSpec(shape, lambda i: (0,) * len(shape))


def cost(flops, nbytes):
    return pl.CostEstimate(flops=int(flops), bytes_accessed=int(nbytes), transcendentals=0)


def select(where, ids, gates, tokens, grads, latent):
    tok, d = tokens.shape
    wide = d // STEPS
    width = latent.shape[2] // 2
    col = lambda rows: pl.BlockSpec((rows, wide), lambda i: (0, i))
    chunk = jax.ShapeDtypeStruct((SLOT, d), BF)
    table = jax.ShapeDtypeStruct((tok, tok), BF)
    half = jax.ShapeDtypeStruct((tok, width), BF)
    return pl.pallas_call(
        select_kernel,
        grid=(STEPS,),
        in_specs=[
            pl.BlockSpec(memory_space=pltpu.SMEM),
            whole(ids.shape),
            whole(gates.shape),
            col(tok),
            col(tok),
            whole(latent.shape),
        ],
        out_specs=[col(SLOT)] * 4 + [whole((tok, tok))] * 3 + [whole((tok, width))] * 2,
        out_shape=[chunk] * 4 + [table] * 3 + [half] * 2,
        scratch_shapes=[pltpu.VMEM((2 * SLOT, tok), BF), pltpu.VMEM((2 * SLOT, tok), F32)],
        cost_estimate=cost(4 * 2 * SLOT * tok * d, 4 * tok * d),
        name="select",
    )(where, ids, gates, tokens, grads, latent)


def latent_kernel(tok_ref, mine_ref, got_ref, out_ref):
    both = (mine_ref[...].astype(F32) + got_ref[...].astype(F32)).astype(BF)
    part = lax.dot_general(
        tok_ref[...], both, (((0,), (0,)), ((), ())), preferred_element_type=F32
    )
    out_ref[...] = part.astype(BF)


def latent_part(tokens, mine, got):
    tok, d = tokens.shape
    width = mine.shape[1]
    wide = d // 7
    return pl.pallas_call(
        latent_kernel,
        grid=(7,),
        in_specs=[
            pl.BlockSpec((tok, wide), lambda i: (0, i)),
            whole((tok, width)),
            whole((tok, width)),
        ],
        out_specs=pl.BlockSpec((wide, width), lambda i: (i, 0)),
        out_shape=jax.ShapeDtypeStruct((d, width), BF),
        cost_estimate=cost(2 * tok * d * width, 2 * tok * d + 2 * d * width),
        name="latent_part",
    )(tokens, mine, got)


def forward_kernel(
    rows_ref, wg, wu, wg2, wu2, wd, wd2, kept, sent, fa, fb, acc, hidden
):
    i = pl.program_id(0)
    f = wg.shape[1]

    @pl.when(i == 0)
    def _():
        acc[...] = jnp.zeros_like(acc)

    @pl.when(i < STEPS)
    def _():
        rows = rows_ref[...]
        acc[:, :f] += dot(rows, wg[...])
        acc[:, f : 2 * f] += dot(rows, wg2[...])
        acc[:, 2 * f : 3 * f] += dot(rows, wu[...])
        acc[:, 3 * f :] += dot(rows, wu2[...])

    @pl.when(i == STEPS - 1)
    def _():
        gate, up = acc[:, : 2 * f], acc[:, 2 * f :]
        sg = jax.nn.sigmoid(gate)
        hidden[...] = (gate * sg * up).astype(BF)
        fa[...] = up * sg * (1.0 + gate * (1.0 - sg))
        fb[...] = gate * sg

    @pl.when(i >= STEPS)
    def _():
        out = dot(hidden[:, :f], wd[...]) + dot(hidden[:, f:], wd2[...])
        out = out.astype(BF)
        half = out.shape[0] // 2
        kept[...] = out[:half]
        sent[...] = out[half:]


def forward(rows, wg, wu, wg2, wu2, wd, wd2):
    n, d = rows.shape
    f = wg.shape[1]
    wide = d // STEPS
    early = lambda i: jnp.minimum(i, STEPS - 1)
    late = lambda i: jnp.maximum(i - STEPS, 0)
    weight = pl.BlockSpec((wide, f), lambda i: (early(i), 0))
    down = pl.BlockSpec((f, wide), lambda i: (0, late(i)))
    out = pl.BlockSpec((n // 2, wide), lambda i: (0, late(i)))
    return pl.pallas_call(
        forward_kernel,
        grid=(2 * STEPS,),
        in_specs=[pl.BlockSpec((n, wide), lambda i: (0, early(i)))] + [weight] * 4 + [down] * 2,
        out_specs=[out] * 2 + [whole((n, 2 * f))] * 2,
        out_shape=[jax.ShapeDtypeStruct((n // 2, d), BF)] * 2
        + [jax.ShapeDtypeStruct((n, 2 * f), F32)] * 2,
        scratch_shapes=[pltpu.VMEM((n, 4 * f), F32), pltpu.VMEM((n, 2 * f), BF)],
        cost_estimate=cost(12 * n * d * f, 12 * d * f + 4 * n * d),
        name="forward",
    )(rows, wg, wu, wg2, wu2, wd, wd2)


def backward_kernel(
    rows_ref, fa, fb, wd, wd2, wg, wu, wg2, wu2, kept, sent, acc, gate_grad, up_grad
):
    i = pl.program_id(0)
    f = wg.shape[1]

    @pl.when(i == 0)
    def _():
        acc[...] = jnp.zeros_like(acc)

    @pl.when(i < STEPS)
    def _():
        rows = rows_ref[...]
        acc[:, :f] += tdot(rows, wd[...])
        acc[:, f:] += tdot(rows, wd2[...])

    @pl.when(i == STEPS - 1)
    def _():
        gate_grad[...] = (acc[...] * fa[...]).astype(BF)
        up_grad[...] = (acc[...] * fb[...]).astype(BF)

    @pl.when(i >= STEPS)
    def _():
        out = tdot(gate_grad[:, :f], wg[...]) + tdot(gate_grad[:, f:], wg2[...])
        out = out + tdot(up_grad[:, :f], wu[...]) + tdot(up_grad[:, f:], wu2[...])
        out = out.astype(BF)
        half = out.shape[0] // 2
        kept[...] = out[:half]
        sent[...] = out[half:]


def backward(rows, fa, fb, wd, wd2, wg, wu, wg2, wu2):
    n, d = rows.shape
    f = wg.shape[1]
    wide = d // STEPS
    early = lambda i: jnp.minimum(i, STEPS - 1)
    late = lambda i: jnp.maximum(i - STEPS, 0)
    weight = pl.BlockSpec((wide, f), lambda i: (late(i), 0))
    down = pl.BlockSpec((f, wide), lambda i: (0, early(i)))
    out = pl.BlockSpec((n // 2, wide), lambda i: (0, late(i)))
    return pl.pallas_call(
        backward_kernel,
        grid=(2 * STEPS,),
        in_specs=[pl.BlockSpec((n, wide), lambda i: (0, early(i)))]
        + [whole((n, 2 * f))] * 2
        + [down] * 2
        + [weight] * 4,
        out_specs=[out] * 2,
        out_shape=[jax.ShapeDtypeStruct((n // 2, d), BF)] * 2,
        scratch_shapes=[
            pltpu.VMEM((n, 2 * f), F32),
            pltpu.VMEM((n, 2 * f), BF),
            pltpu.VMEM((n, 2 * f), BF),
        ],
        cost_estimate=cost(12 * n * d * f, 12 * d * f + 4 * n * d),
        name="backward",
    )(rows, fa, fb, wd, wd2, wg, wu, wg2, wu2)


def combine_kernel(n_tables, *refs):
    tables, parts, out = refs[:n_tables], refs[n_tables:-1], refs[-1]
    back = jnp.concatenate([part[...] for part in parts], axis=0)
    total = dot(tables[0][...], back)
    for table in tables[1:]:
        total = total + dot(table[...], back)
    out[...] = total.astype(BF)


def combine(tables, parts):
    tok = tables[0].shape[0]
    d = parts[0].shape[1]
    wide = d // STEPS
    col = lambda rows: pl.BlockSpec((rows, wide), lambda i: (0, i))
    return pl.pallas_call(
        functools.partial(combine_kernel, len(tables)),
        grid=(STEPS,),
        in_specs=[whole((tok, tok))] * len(tables) + [col(part.shape[0]) for part in parts],
        out_specs=col(tok),
        out_shape=jax.ShapeDtypeStruct((tok, d), BF),
        cost_estimate=cost(2 * tok * tok * d * len(tables), 4 * tok * d),
        name="combine",
    )(*tables, *parts)


def per_device(tokens, route_ids, route_gates, w_gate, w_up, w_down, out_grad, latent_grad):
    p = lax.axis_index("pipe")
    s = lax.axis_index("expert")
    where = jnp.stack([p, s]).astype(jnp.int32)
    wg, wu, wd = w_gate[0], w_up[0], w_down[0]
    wg2, wu2, wd2 = across(wg, CORE), across(wu, CORE), across(wd, CORE)
    mirror = [(i, 15 - i) for i in range(16)]

    send0, send1, dsend0, dsend1, sel, hi, lo, mine, other = select(
        where, route_ids, route_gates, tokens, out_grad, latent_grad
    )
    got = lax.ppermute(other, "pipe", mirror)
    part = latent_part(tokens, mine, got)
    share = lax.psum_scatter(part, "expert", scatter_dimension=0, tiled=True)
    theirs = lax.ppermute(share, "pipe", mirror)
    low = p < 8
    kv_grad = jnp.concatenate(
        [jnp.where(low, share, theirs), jnp.where(low, theirs, share)], axis=1
    )[None]

    rows = dispatch(send0, send1)
    drows = dispatch(dsend0, dsend1)
    kept, sent, fa, fb = forward(rows, wg, wu, wg2, wu2, wd, wd2)
    routed = combine([hi, lo], collect(kept, sent))
    dkept, dsent = backward(drows, fa, fb, wd, wd2, wg, wu, wg2, wu2)
    token_grad = combine([sel], collect(dkept, dsent))
    return routed, token_grad, kv_grad


def solution(mesh):
    return jax.shard_map(
        per_device,
        mesh=mesh,
        in_specs=(
            P("expert", None),
            P("expert", None),
            P("expert", None),
            P("expert", None, "pipe"),
            P("expert", None, "pipe"),
            P("expert", "pipe", None),
            P("expert", None),
            P("pipe", "expert", None),
        ),
        out_specs=(P("expert", None), P("expert", None), P("pipe", "expert", None)),
        check_vma=False,
    )
```

```python
import functools
import jax
import jax.numpy as jnp
from jax import lax
from jax.experimental import pallas as pl
from jax.experimental.pallas import tpu as pltpu
from jax.sharding import PartitionSpec as P

SLOT = 8
BF = jnp.bfloat16
F32 = jnp.float32
CORE, Y_HI, X_LOW = 1, 2, 4
STEPS = 4


def across(value, mask):
    return lax.ppermute(value, "pipe", [(i, i ^ mask) for i in range(16)])


def delta(p, k):
    return (p & 1) * 8 + (k ^ ((p >> 1) & 1)) * 4 + (p >> 2)


def shifted(value, k, mask=0):
    pairs = [
        (p * 16 + e, (p ^ mask) * 16 + (e ^ delta(p, k))) for p in range(16) for e in range(16)
    ]
    return lax.ppermute(value, ("pipe", "expert"), pairs)


def along_x(value, step):
    pairs = []
    for i in range(16):
        hop = 3 if (i & 1) ^ step else 1
        pairs.append((i, i ^ (X_LOW * hop)))
    return lax.ppermute(value, "pipe", pairs)


def dispatch(first, second):
    block = jnp.concatenate([shifted(first, 0), shifted(second, 1)], axis=0)
    two = jnp.concatenate([block, along_x(block, 0)], axis=0)
    return jnp.concatenate([two, along_x(two, 1)], axis=0)


def add(a, b):
    return (a.astype(F32) + b.astype(F32)).astype(BF)


def collect(kept, sent, after=None):
    two = add(kept, along_x(sent, 1))
    size = two.shape[0] // 2
    one = add(two[:size], along_x(two[size:], 0))
    full = add(one[:SLOT], across(one[SLOT:], Y_HI))
    block = jnp.concatenate([shifted(full, 0), shifted(full, 0, Y_HI)], axis=0)
    two = block, along_x(block, 0)
    two = jnp.concatenate(two, axis=0) if after is None else join(*two, after)
    rest = along_x(two, 1)
    return two, rest, across(two, CORE), across(rest, CORE)


def dot(a, b):
    return jnp.dot(a, b, preferred_element_type=F32)


def tdot(a, b):
    return lax.dot_general(a, b, (((1,), (1,)), ((), ())), preferred_element_type=F32)


def far(value):
    return pltpu.with_memory_space_constraint(value, pltpu.HBM)


def near(value):
    return pltpu.with_memory_space_constraint(value, pltpu.VMEM)


def cost(flops, nbytes):
    return pl.CostEstimate(flops=int(flops), bytes_accessed=int(nbytes), transcendentals=0)


def tables(p, s, ids, gates, rows):
    tok = ids.shape[1]
    row = lax.broadcasted_iota(jnp.int32, (rows, tok), 0)
    far_core, k = row >> 6, (row >> 3) & 1
    ring = (row >> 4) & 3
    off = ring ^ (ring >> 1)
    off = off ^ (2 * (off & 1) * ((p & 1) ^ far_core))
    base = s ^ ((p & 1) * 8 + ((p >> 1) & 1) * 4 + (p >> 2))
    expert = base ^ (far_core * 8) ^ (k * 4) ^ off
    named = jnp.zeros((rows, tok), F32)
    gate = jnp.zeros((rows, tok), F32)
    for choice in range(ids.shape[0]):
        hit = ids[choice : choice + 1, :] == expert
        named = jnp.where(hit, 1.0, named)
        gate = jnp.where(hit, gates[choice : choice + 1, :], gate)
    first = lax.broadcasted_iota(jnp.int32, (tok, tok), 0)
    second = lax.broadcasted_iota(jnp.int32, (tok, tok), 1)
    earlier = jnp.where(first < second, 1.0, 0.0).astype(BF)
    before = dot(named.astype(BF), earlier)
    slot = (row & (SLOT - 1)).astype(F32)
    here = jnp.logical_and(named > 0.5, before == slot)
    return jnp.where(here, 1.0, 0.0), jnp.where(here, gate, 0.0)


def select_kernel(
    p_ref, s_ref, ids_ref, gates_ref, tok_ref, grad_ref, lat_ref,
    send0, send1, dsend0, dsend1, mine_ref, other_ref, pick, weight,
):
    @pl.when(pl.program_id(0) == 0)
    def _():
        p, s = p_ref[0], s_ref[0]
        sel, mix = tables(p, s, ids_ref[...], gates_ref[...], 2 * SLOT)
        pick[...] = sel.astype(BF)
        total = jnp.sum(mix, axis=1, keepdims=True)
        weight[...] = jnp.broadcast_to(total, weight.shape)
        lat = lat_ref[0]
        width = lat.shape[1] // 2
        low = p < 8
        mine_ref[...] = jnp.where(low, lat[:, :width], lat[:, width:])
        other_ref[...] = jnp.where(low, lat[:, width:], lat[:, :width])

    rows = dot(pick[...], tok_ref[...]).astype(BF)
    drows = (dot(pick[...], grad_ref[...]) * weight[:, :1]).astype(BF)
    send0[...] = rows[:SLOT]
    send1[...] = rows[SLOT:]
    dsend0[...] = drows[:SLOT]
    dsend1[...] = drows[SLOT:]


def whole(shape):
    return pl.BlockSpec(shape, lambda i: (0,) * len(shape))


SCALAR = pl.BlockSpec(memory_space=pltpu.SMEM)


def select(p, s, ids, gates, tokens, grads, latent):
    tok, d = tokens.shape
    wide = d // STEPS
    width = latent.shape[2] // 2
    col = lambda rows: pl.BlockSpec((rows, wide), lambda i: (0, i))
    chunk = jax.ShapeDtypeStruct((SLOT, d), BF)
    half = jax.ShapeDtypeStruct((tok, width), BF)
    return pl.pallas_call(
        select_kernel,
        grid=(STEPS,),
        in_specs=[
            SCALAR,
            SCALAR,
            whole(ids.shape),
            whole(gates.shape),
            col(tok),
            col(tok),
            whole(latent.shape),
        ],
        out_specs=[col(SLOT)] * 4 + [whole((tok, width))] * 2,
        out_shape=[chunk] * 4 + [half] * 2,
        scratch_shapes=[pltpu.VMEM((2 * SLOT, tok), BF), pltpu.VMEM((2 * SLOT, tok), F32)],
        cost_estimate=cost(4 * 2 * SLOT * tok * d, 4 * tok * d),
        compiler_params=pltpu.CompilerParams(vmem_limit_bytes=16 << 20),
        name="select",
    )(p, s, ids, gates, far(tokens), far(grads), far(latent))


def latent_kernel(
    p_ref, s_ref, ids_ref, gates_ref, mine_ref, got_ref, tok_ref,
    out_ref, sel_ref, hi_ref, lo_ref, turned,
):
    i = pl.program_id(0)

    @pl.when(i == 0)
    def _():
        tok = ids_ref.shape[1]
        sel, mix = tables(p_ref[0], s_ref[0], ids_ref[...], gates_ref[...], tok)
        sel_ref[...] = sel.T.astype(BF)
        mix = mix.T
        hi = mix.astype(BF)
        hi_ref[...] = hi
        lo_ref[...] = (mix - hi.astype(F32)).astype(BF)
        turned[...] = (mine_ref[...].astype(F32) + got_ref[...].astype(F32)).astype(BF)

    part = lax.dot_general(tok_ref[...], turned[...], (((0,), (0,)), ((), ())), preferred_element_type=F32)
    out_ref[...] = part.astype(BF)


def latent_part(p, s, ids, gates, mine, got, tokens):
    tok, d = tokens.shape
    width = mine.shape[1]
    n = 16
    group = 4
    table = jax.ShapeDtypeStruct((tok, tok), BF)
    return pl.pallas_call(
        latent_kernel,
        grid=(n // group,),
        in_specs=[
            SCALAR,
            SCALAR,
            whole(ids.shape),
            whole(gates.shape),
            whole(mine.shape),
            whole(got.shape),
            pl.BlockSpec((tok, d // n * group), lambda i: (0, i)),
        ],
        out_specs=[pl.BlockSpec((d // n * group, width), lambda i: (i, 0))]
        + [whole((tok, tok))] * 3,
        out_shape=[pltpu.HBM((d, width), BF)] + [table] * 3,
        scratch_shapes=[pltpu.VMEM((tok, width), BF)],
        cost_estimate=cost(2 * tok * d * width, 2 * tok * d + 2 * d * width),
        compiler_params=pltpu.CompilerParams(vmem_limit_bytes=16 << 20),
        name="latent_part",
    )(p, s, ids, gates, mine, got, tokens)


def finish_kernel(p_ref, share_ref, theirs_ref, out_ref):
    low = p_ref[0] < 8
    share, theirs = share_ref[...], theirs_ref[...]
    width = share.shape[1]
    out_ref[0, :, :width] = jnp.where(low, share, theirs)
    out_ref[0, :, width:] = jnp.where(low, theirs, share)


def finish(p, share, theirs):
    rows, width = share.shape
    return pl.pallas_call(
        finish_kernel,
        in_specs=[SCALAR] + [pl.BlockSpec(memory_space=pltpu.VMEM)] * 2,
        out_specs=pl.BlockSpec(memory_space=pltpu.VMEM),
        out_shape=jax.ShapeDtypeStruct((1, rows, 2 * width), BF),
        cost_estimate=cost(0, 8 * width * rows),
        compiler_params=pltpu.CompilerParams(vmem_limit_bytes=8 << 20),
        name="finish",
    )(p, share, theirs)


def join_kernel(a, b, _, out):
    size = a.shape[0]
    out[:size] = a[...]
    out[size:] = b[...]


def join(a, b, after):
    vmem = pl.BlockSpec(memory_space=pltpu.VMEM)
    return pl.pallas_call(
        join_kernel,
        in_specs=[vmem] * 2 + [pl.BlockSpec(memory_space=pl.ANY)],
        out_specs=vmem,
        out_shape=pltpu.VMEM((2 * a.shape[0], a.shape[1]), a.dtype),
        cost_estimate=cost(0, 8 * a.size),
        compiler_params=pltpu.CompilerParams(vmem_limit_bytes=8 << 20),
        name="join",
    )(near(a), near(b), after)


PIECES = 7


def forward_kernel(rows, wg, wu, wg2, wu2, wd, wd2, _, kept, sent, fa, fb):
    n, d = rows.shape
    f = wg.shape[1]
    wide = d // PIECES
    acc = jnp.zeros((n, 4 * f), F32)
    for i in range(PIECES):
        at = pl.ds(i * wide, wide)
        weights = jnp.concatenate([wg[at, :], wg2[at, :], wu[at, :], wu2[at, :]], axis=1)
        acc = acc + dot(rows[:, at], weights)
    gate, up = acc[:, : 2 * f], acc[:, 2 * f :]
    sg = jax.nn.sigmoid(gate)
    hidden = (gate * sg * up).astype(BF)
    fa[...] = up * sg * (1.0 + gate * (1.0 - sg))
    fb[...] = gate * sg
    for i in range(PIECES):
        at = pl.ds(i * wide, wide)
        out = dot(hidden, jnp.concatenate([wd[:, at], wd2[:, at]], axis=0)).astype(BF)
        kept[:, at] = out[: n // 2]
        sent[:, at] = out[n // 2 :]


def forward(rows, wg, wu, wg2, wu2, wd, wd2, after):
    n, d = rows.shape
    f = wg.shape[1]
    vmem = pl.BlockSpec(memory_space=pltpu.VMEM)
    return pl.pallas_call(
        forward_kernel,
        in_specs=[vmem] * 7 + [pl.BlockSpec(memory_space=pl.ANY)],
        out_specs=[vmem] * 4,
        out_shape=[pltpu.VMEM((n // 2, d), BF)] * 2 + [pltpu.VMEM((n, 2 * f), F32)] * 2,
        cost_estimate=cost(12 * n * d * f, 12 * d * f + 4 * n * d),
        compiler_params=pltpu.CompilerParams(vmem_limit_bytes=12 << 20),
        name="forward",
    )(*map(near, (rows, wg, wu, wg2, wu2, wd, wd2)), after)


def backward_kernel(rows, fa, fb, wd, wd2, wg, wu, wg2, wu2, kept, sent):
    n, d = rows.shape
    f = wg.shape[1]
    wide = d // PIECES
    acc = jnp.zeros((n, 2 * f), F32)
    for i in range(PIECES):
        at = pl.ds(i * wide, wide)
        acc = acc + tdot(rows[:, at], jnp.concatenate([wd[:, at], wd2[:, at]], axis=0))
    grads = jnp.concatenate([(acc * fa[...]).astype(BF), (acc * fb[...]).astype(BF)], axis=1)
    for i in range(PIECES):
        at = pl.ds(i * wide, wide)
        weights = jnp.concatenate([wg[at, :], wg2[at, :], wu[at, :], wu2[at, :]], axis=1)
        out = tdot(grads, weights).astype(BF)
        kept[:, at] = out[: n // 2]
        sent[:, at] = out[n // 2 :]


def backward(rows, fa, fb, wd, wd2, wg, wu, wg2, wu2):
    n, d = rows.shape
    f = wg.shape[1]
    vmem = pl.BlockSpec(memory_space=pltpu.VMEM)
    return pl.pallas_call(
        backward_kernel,
        in_specs=[vmem] * 9,
        out_specs=[vmem] * 2,
        out_shape=[pltpu.VMEM((n // 2, d), BF)] * 2,
        cost_estimate=cost(12 * n * d * f, 12 * d * f + 4 * n * d),
        compiler_params=pltpu.CompilerParams(vmem_limit_bytes=12 << 20),
        name="backward",
    )(*map(near, (rows, fa, fb, wd, wd2, wg, wu, wg2, wu2)))


def combine_kernel(n_tables, *refs):
    mixing, parts, out, buf, sems = refs[:n_tables], refs[n_tables:-3], *refs[-3:]
    d = out.shape[1]
    wide = d // PIECES
    copies = []
    for i in range(PIECES):
        at = pl.ds(i * wide, wide)
        back = jnp.concatenate([part[:, at] for part in parts], axis=0)
        total = dot(mixing[0][...], back)
        for table in mixing[1:]:
            total = total + dot(table[...], back)
        buf[:, at] = total.astype(BF)
        copy = pltpu.make_async_copy(buf.at[:, at], out.at[:, at], sems.at[i])
        copy.start()
        copies.append(copy)
    for copy in copies:
        copy.wait()


def combine(mixing, parts):
    tok = mixing[0].shape[0]
    d = parts[0].shape[1]
    vmem = pl.BlockSpec(memory_space=pltpu.VMEM)
    return pl.pallas_call(
        functools.partial(combine_kernel, len(mixing)),
        in_specs=[vmem] * (len(mixing) + len(parts)),
        out_specs=pl.BlockSpec(memory_space=pl.ANY),
        out_shape=jax.ShapeDtypeStruct((tok, d), BF),
        scratch_shapes=[pltpu.VMEM((tok, d), BF), pltpu.SemaphoreType.DMA((PIECES,))],
        cost_estimate=cost(2 * tok * tok * d * len(mixing), 4 * tok * d),
        compiler_params=pltpu.CompilerParams(vmem_limit_bytes=12 << 20),
        name="combine",
    )(*map(near, mixing), *map(near, parts))


def per_device(tokens, route_ids, route_gates, w_gate, w_up, w_down, out_grad, latent_grad):
    p = lax.axis_index("pipe").reshape(1).astype(jnp.int32)
    s = lax.axis_index("expert").reshape(1).astype(jnp.int32)
    ids, gates = route_ids.T, route_gates.T
    wg, wu, wd = w_gate[0], w_up[0], w_down[0]
    wg2, wu2, wd2 = across(wg, CORE), across(wu, CORE), across(wd, CORE)
    mirror = [(i, 15 - i) for i in range(16)]

    send0, send1, dsend0, dsend1, mine, other = select(
        p, s, ids, gates, tokens, out_grad, latent_grad
    )
    got = lax.ppermute(other, "pipe", mirror)
    part, sel, hi, lo = latent_part(p, s, ids, gates, mine, got, tokens)
    share = lax.psum_scatter(part, "expert", scatter_dimension=0, tiled=True)
    theirs = lax.ppermute(share, "pipe", mirror)
    kv_grad = finish(p, share, theirs)

    rows = dispatch(send0, send1)
    drows = dispatch(dsend0, dsend1)
    kept, sent, fa, fb = forward(rows, wg, wu, wg2, wu2, wd, wd2, hi)
    routed = combine([hi, lo], collect(kept, sent))
    dkept, dsent = backward(drows, fa, fb, wd, wd2, wg, wu, wg2, wu2)
    token_grad = combine([sel], collect(dkept, dsent, share))
    return routed, token_grad, kv_grad


def solution(mesh):
    return jax.shard_map(
        per_device,
        mesh=mesh,
        in_specs=(
            P("expert", None),
            P("expert", None),
            P("expert", None),
            P("expert", None, "pipe"),
            P("expert", None, "pipe"),
            P("expert", "pipe", None),
            P("expert", None),
            P("pipe", "expert", None),
        ),
        out_specs=(P("expert", None), P("expert", None), P("pipe", "expert", None)),
        check_vma=False,
    )
```

```python
import functools
import jax
import jax.numpy as jnp
from jax import lax
from jax.experimental import pallas as pl
from jax.experimental.pallas import tpu as pltpu
from jax.sharding import PartitionSpec as P

SLOT = 8
BF = jnp.bfloat16
F32 = jnp.float32
CORE, Y_HI, X_LOW = 1, 2, 4
STEPS = 4


def across(value, mask):
    return lax.ppermute(value, "pipe", [(i, i ^ mask) for i in range(16)])


def delta(p, k):
    return (p & 1) * 8 + (k ^ ((p ^ (p >> 1)) & 1)) * 4 + (p >> 2)


def shifted(value, k):
    pairs = [(p * 16 + e, p * 16 + (e ^ delta(p, k))) for p in range(16) for e in range(16)]
    return lax.ppermute(value, ("pipe", "expert"), pairs)


def along_x(value, step):
    pairs = []
    for i in range(16):
        hop = 3 if (i & 1) ^ step else 1
        pairs.append((i, i ^ (X_LOW * hop)))
    return lax.ppermute(value, "pipe", pairs)


def dispatch(first, second):
    block = jnp.concatenate([shifted(first, 0), shifted(second, 1)], axis=0)
    two = jnp.concatenate([block, along_x(block, 0)], axis=0)
    return jnp.concatenate([two, along_x(two, 1)], axis=0)


def add(a, b):
    return (a.astype(F32) + b.astype(F32)).astype(BF)


def collect(kept, sent, after=None, last=None):
    two = add(kept, along_x(sent, 1))
    size = two.shape[0] // 2
    one = add(two[:size], along_x(two[size:], 0))
    full = add(one[:SLOT], across(one[SLOT:], Y_HI))
    chunk = shifted(full, 0)
    block = jnp.concatenate([chunk, across(chunk, Y_HI)], axis=0)
    two = block, along_x(block, 0)
    two = jnp.concatenate(two, axis=0) if after is None else join(*two, after)
    rest = along_x(two, 1)
    if last is not None:
        rest = later(rest, last)
    return two, rest, across(two, CORE), across(rest, CORE)


def dot(a, b):
    return jnp.dot(a, b, preferred_element_type=F32)


def tdot(a, b):
    return lax.dot_general(a, b, (((1,), (1,)), ((), ())), preferred_element_type=F32)


def far(value):
    return pltpu.with_memory_space_constraint(value, pltpu.HBM)


def near(value):
    return pltpu.with_memory_space_constraint(value, pltpu.VMEM)


def cost(flops, nbytes):
    return pl.CostEstimate(flops=int(flops), bytes_accessed=int(nbytes), transcendentals=0)


def tables(p, s, ids, gates, rows):
    tok = ids.shape[1]
    row = lax.broadcasted_iota(jnp.int32, (rows, tok), 0)
    far_core, k = row >> 6, (row >> 3) & 1
    ring = (row >> 4) & 3
    off = ring ^ (ring >> 1)
    off = off ^ (2 * (off & 1) * ((p & 1) ^ far_core))
    expert = s ^ delta(p, 0) ^ (far_core * 12) ^ (k * 4) ^ off
    named = jnp.zeros((rows, tok), F32)
    gate = jnp.zeros((rows, tok), F32)
    for choice in range(ids.shape[0]):
        hit = ids[choice : choice + 1, :] == expert
        named = jnp.where(hit, 1.0, named)
        gate = jnp.where(hit, gates[choice : choice + 1, :], gate)
    first = lax.broadcasted_iota(jnp.int32, (tok, tok), 0)
    second = lax.broadcasted_iota(jnp.int32, (tok, tok), 1)
    earlier = jnp.where(first < second, 1.0, 0.0).astype(BF)
    before = dot(named.astype(BF), earlier)
    slot = (row & (SLOT - 1)).astype(F32)
    here = jnp.logical_and(named > 0.5, before == slot)
    return jnp.where(here, 1.0, 0.0), jnp.where(here, gate, 0.0)


def select_kernel(
    p_ref, s_ref, ids_ref, gates_ref, tok_ref, grad_ref,
    send0, send1, dsend0, dsend1, pick, weight,
):
    @pl.when(pl.program_id(0) == 0)
    def _():
        p, s = p_ref[0], s_ref[0]
        sel, mix = tables(p, s, ids_ref[...], gates_ref[...], 2 * SLOT)
        pick[...] = sel.astype(BF)
        total = jnp.sum(mix, axis=1, keepdims=True)
        weight[...] = jnp.broadcast_to(total, weight.shape)
    rows = dot(pick[...], tok_ref[...]).astype(BF)
    drows = (dot(pick[...], grad_ref[...]) * weight[:, :1]).astype(BF)
    send0[...] = rows[:SLOT]
    send1[...] = rows[SLOT:]
    dsend0[...] = drows[:SLOT]
    dsend1[...] = drows[SLOT:]


def whole(shape):
    return pl.BlockSpec(shape, lambda i: (0,) * len(shape))


SCALAR = pl.BlockSpec(memory_space=pltpu.SMEM)


def select(p, s, ids, gates, tokens, grads):
    tok, d = tokens.shape
    wide = d // STEPS
    col = lambda rows: pl.BlockSpec((rows, wide), lambda i: (0, i))
    chunk = jax.ShapeDtypeStruct((SLOT, d), BF)
    return pl.pallas_call(
        select_kernel,
        grid=(STEPS,),
        in_specs=[
            SCALAR,
            SCALAR,
            whole(ids.shape),
            whole(gates.shape),
            col(tok),
            col(tok),
        ],
        out_specs=[col(SLOT)] * 4,
        out_shape=[chunk] * 4,
        scratch_shapes=[pltpu.VMEM((2 * SLOT, tok), BF), pltpu.VMEM((2 * SLOT, tok), F32)],
        cost_estimate=cost(4 * 2 * SLOT * tok * d, 4 * tok * d),
        compiler_params=pltpu.CompilerParams(vmem_limit_bytes=16 << 20),
        name="select",
    )(p, s, ids, gates, far(tokens), far(grads))


def latent_kernel(
    p_ref, s_ref, ids_ref, gates_ref, lat_ref, got_ref, tok_ref,
    out_ref, sel_ref, hi_ref, lo_ref, turned,
):
    i = pl.program_id(0)

    @pl.when(i == 0)
    def _():
        tok = ids_ref.shape[1]
        sel, mix = tables(p_ref[0], s_ref[0], ids_ref[...], gates_ref[...], tok)
        sel_ref[...] = sel.T.astype(BF)
        mix = mix.T
        hi = mix.astype(BF)
        hi_ref[...] = hi
        lo_ref[...] = (mix - hi.astype(F32)).astype(BF)
        width = got_ref.shape[1]
        mine = jnp.where(p_ref[0] < 8, lat_ref[0, :, :width], lat_ref[0, :, width:])
        turned[...] = (mine.astype(F32) + got_ref[...].astype(F32)).astype(BF)

    part = lax.dot_general(tok_ref[...], turned[...], (((0,), (0,)), ((), ())), preferred_element_type=F32)
    out_ref[...] = part.astype(BF)


def latent_part(p, s, ids, gates, latent, got, tokens):
    tok, d = tokens.shape
    width = got.shape[1]
    n = 16
    group = 4
    table = jax.ShapeDtypeStruct((tok, tok), BF)
    return pl.pallas_call(
        latent_kernel,
        grid=(n // group,),
        in_specs=[
            SCALAR,
            SCALAR,
            whole(ids.shape),
            whole(gates.shape),
            whole(latent.shape),
            whole(got.shape),
            pl.BlockSpec((tok, d // n * group), lambda i: (0, i)),
        ],
        out_specs=[pl.BlockSpec((d // n * group, width), lambda i: (i, 0))]
        + [whole((tok, tok))] * 3,
        out_shape=[pltpu.HBM((d, width), BF)] + [table] * 3,
        scratch_shapes=[pltpu.VMEM((tok, width), BF)],
        cost_estimate=cost(2 * tok * d * width, 2 * tok * d + 2 * d * width),
        compiler_params=pltpu.CompilerParams(vmem_limit_bytes=16 << 20),
        name="latent_part",
    )(p, s, ids, gates, latent, got, tokens)


def finish_kernel(p_ref, share_ref, theirs_ref, out_ref):
    low = p_ref[0] < 8
    share, theirs = share_ref[...], theirs_ref[...]
    width = share.shape[1]
    out_ref[0, :, :width] = jnp.where(low, share, theirs)
    out_ref[0, :, width:] = jnp.where(low, theirs, share)


def finish(p, share, theirs):
    rows, width = share.shape
    return pl.pallas_call(
        finish_kernel,
        in_specs=[SCALAR] + [pl.BlockSpec(memory_space=pltpu.VMEM)] * 2,
        out_specs=pl.BlockSpec(memory_space=pltpu.VMEM),
        out_shape=jax.ShapeDtypeStruct((1, rows, 2 * width), BF),
        cost_estimate=cost(0, 8 * width * rows),
        compiler_params=pltpu.CompilerParams(vmem_limit_bytes=8 << 20),
        name="finish",
    )(p, share, theirs)


def join_kernel(a, b, _, out):
    size = a.shape[0]
    out[:size] = a[...]
    out[size:] = b[...]


def pass_kernel(a, _, out):
    out[...] = a[...]


def later(a, after):
    vmem = pl.BlockSpec(memory_space=pltpu.VMEM)
    return pl.pallas_call(
        pass_kernel,
        in_specs=[vmem, pl.BlockSpec(memory_space=pl.ANY)],
        out_specs=vmem,
        out_shape=pltpu.VMEM(a.shape, a.dtype),
        cost_estimate=cost(0, 4 * a.size),
        compiler_params=pltpu.CompilerParams(vmem_limit_bytes=8 << 20),
        name="later",
    )(near(a), after)


def join(a, b, after):
    vmem = pl.BlockSpec(memory_space=pltpu.VMEM)
    return pl.pallas_call(
        join_kernel,
        in_specs=[vmem] * 2 + [pl.BlockSpec(memory_space=pl.ANY)],
        out_specs=vmem,
        out_shape=pltpu.VMEM((2 * a.shape[0], a.shape[1]), a.dtype),
        cost_estimate=cost(0, 8 * a.size),
        compiler_params=pltpu.CompilerParams(vmem_limit_bytes=8 << 20),
        name="join",
    )(near(a), near(b), after)


PIECES = 7


def forward_kernel(rows, wg, wu, wg2, wu2, wd, wd2, _, kept, sent, fa, fb):
    n, d = rows.shape
    f = wg.shape[1]
    wide = d // PIECES
    acc = jnp.zeros((n, 4 * f), F32)
    for i in range(PIECES):
        at = pl.ds(i * wide, wide)
        weights = jnp.concatenate([wg[at, :], wg2[at, :], wu[at, :], wu2[at, :]], axis=1)
        acc = acc + dot(rows[:, at], weights)
    gate, up = acc[:, : 2 * f], acc[:, 2 * f :]
    sg = jax.nn.sigmoid(gate)
    hidden = (gate * sg * up).astype(BF)
    fa[...] = up * sg * (1.0 + gate * (1.0 - sg))
    fb[...] = gate * sg
    for i in range(PIECES):
        at = pl.ds(i * wide, wide)
        out = dot(hidden, jnp.concatenate([wd[:, at], wd2[:, at]], axis=0)).astype(BF)
        kept[:, at] = out[: n // 2]
        sent[:, at] = out[n // 2 :]


def forward(rows, wg, wu, wg2, wu2, wd, wd2, after):
    n, d = rows.shape
    f = wg.shape[1]
    vmem = pl.BlockSpec(memory_space=pltpu.VMEM)
    return pl.pallas_call(
        forward_kernel,
        in_specs=[vmem] * 7 + [pl.BlockSpec(memory_space=pl.ANY)],
        out_specs=[vmem] * 4,
        out_shape=[pltpu.VMEM((n // 2, d), BF)] * 2 + [pltpu.VMEM((n, 2 * f), F32)] * 2,
        cost_estimate=cost(12 * n * d * f, 12 * d * f + 4 * n * d),
        compiler_params=pltpu.CompilerParams(vmem_limit_bytes=12 << 20),
        name="forward",
    )(*map(near, (rows, wg, wu, wg2, wu2, wd, wd2)), after)


def backward_kernel(rows, fa, fb, wd, wd2, wg, wu, wg2, wu2, kept, sent):
    n, d = rows.shape
    f = wg.shape[1]
    wide = d // PIECES
    acc = jnp.zeros((n, 2 * f), F32)
    for i in range(PIECES):
        at = pl.ds(i * wide, wide)
        acc = acc + tdot(rows[:, at], jnp.concatenate([wd[:, at], wd2[:, at]], axis=0))
    grads = jnp.concatenate([(acc * fa[...]).astype(BF), (acc * fb[...]).astype(BF)], axis=1)
    for i in range(PIECES):
        at = pl.ds(i * wide, wide)
        weights = jnp.concatenate([wg[at, :], wg2[at, :], wu[at, :], wu2[at, :]], axis=1)
        out = tdot(grads, weights).astype(BF)
        kept[:, at] = out[: n // 2]
        sent[:, at] = out[n // 2 :]


def backward(rows, fa, fb, wd, wd2, wg, wu, wg2, wu2):
    n, d = rows.shape
    f = wg.shape[1]
    vmem = pl.BlockSpec(memory_space=pltpu.VMEM)
    return pl.pallas_call(
        backward_kernel,
        in_specs=[vmem] * 9,
        out_specs=[vmem] * 2,
        out_shape=[pltpu.VMEM((n // 2, d), BF)] * 2,
        cost_estimate=cost(12 * n * d * f, 12 * d * f + 4 * n * d),
        compiler_params=pltpu.CompilerParams(vmem_limit_bytes=12 << 20),
        name="backward",
    )(*map(near, (rows, fa, fb, wd, wd2, wg, wu, wg2, wu2)))


def combine_kernel(n_tables, *refs):
    mixing, parts, out, buf, sems = refs[:n_tables], refs[n_tables:-3], *refs[-3:]
    d = out.shape[1]
    wide = d // PIECES
    copies = []
    for i in range(PIECES):
        at = pl.ds(i * wide, wide)
        back = jnp.concatenate([part[:, at] for part in parts], axis=0)
        total = dot(mixing[0][...], back)
        for table in mixing[1:]:
            total = total + dot(table[...], back)
        buf[:, at] = total.astype(BF)
        copy = pltpu.make_async_copy(buf.at[:, at], out.at[:, at], sems.at[i])
        copy.start()
        copies.append(copy)
    for copy in copies:
        copy.wait()


def combine(mixing, parts):
    tok = mixing[0].shape[0]
    d = parts[0].shape[1]
    vmem = pl.BlockSpec(memory_space=pltpu.VMEM)
    return pl.pallas_call(
        functools.partial(combine_kernel, len(mixing)),
        in_specs=[vmem] * (len(mixing) + len(parts)),
        out_specs=pl.BlockSpec(memory_space=pl.ANY),
        out_shape=jax.ShapeDtypeStruct((tok, d), BF),
        scratch_shapes=[pltpu.VMEM((tok, d), BF), pltpu.SemaphoreType.DMA((PIECES,))],
        cost_estimate=cost(2 * tok * tok * d * len(mixing), 4 * tok * d),
        compiler_params=pltpu.CompilerParams(vmem_limit_bytes=12 << 20),
        name="combine",
    )(*map(near, mixing), *map(near, parts))


def per_device(tokens, route_ids, route_gates, w_gate, w_up, w_down, out_grad, latent_grad):
    p = lax.axis_index("pipe").reshape(1).astype(jnp.int32)
    s = lax.axis_index("expert").reshape(1).astype(jnp.int32)
    ids, gates = route_ids.T, route_gates.T
    wg, wu, wd = w_gate[0], w_up[0], w_down[0]
    wg2, wu2, wd2 = across(wg, CORE), across(wu, CORE), across(wd, CORE)
    mirror = [(i, 15 - i) for i in range(16)]

    send0, send1, dsend0, dsend1 = select(p, s, ids, gates, tokens, out_grad)
    latent = latent_grad[0]
    width = latent.shape[1] // 2
    other = jnp.where(p[0] < 8, latent[:, width:], latent[:, :width])
    got = lax.ppermute(other, "pipe", mirror)
    send0 = later(send0, got)
    part, sel, hi, lo = latent_part(p, s, ids, gates, latent_grad, got, tokens)
    share = lax.psum_scatter(part, "expert", scatter_dimension=0, tiled=True)
    theirs = lax.ppermute(share, "pipe", mirror)
    kv_grad = finish(p, share, theirs)

    rows = dispatch(send0, send1)
    drows = dispatch(dsend0, dsend1)
    kept, sent, fa, fb = forward(rows, wg, wu, wg2, wu2, wd, wd2, hi)
    routed = combine([hi, lo], collect(kept, sent))
    dkept, dsent = backward(drows, fa, fb, wd, wd2, wg, wu, wg2, wu2)
    token_grad = combine([sel], collect(dkept, dsent, share, theirs))
    return routed, token_grad, kv_grad


def solution(mesh):
    return jax.shard_map(
        per_device,
        mesh=mesh,
        in_specs=(
            P("expert", None),
            P("expert", None),
            P("expert", None),
            P("expert", None, "pipe"),
            P("expert", None, "pipe"),
            P("expert", "pipe", None),
            P("expert", None),
            P("pipe", "expert", None),
        ),
        out_specs=(P("expert", None), P("expert", None), P("pipe", "expert", None)),
        check_vma=False,
    )
```

```python
import functools
import jax
import jax.numpy as jnp
from jax import lax
from jax.experimental import pallas as pl
from jax.experimental.pallas import tpu as pltpu
from jax.sharding import PartitionSpec as P

SLOT = 8
BF = jnp.bfloat16
F32 = jnp.float32
CORE, Y_HI, X_LOW = 1, 2, 4
STEPS = 4


def across(value, mask):
    return lax.ppermute(value, "pipe", [(i, i ^ mask) for i in range(16)])


def delta(p, k):
    return (p & 1) * 8 + (k ^ ((p ^ (p >> 1)) & 1)) * 4 + (p >> 2)


def shifted(value, k):
    pairs = [(p * 16 + e, p * 16 + (e ^ delta(p, k))) for p in range(16) for e in range(16)]
    return lax.ppermute(value, ("pipe", "expert"), pairs)


def along_x(value, step):
    pairs = []
    for i in range(16):
        hop = 3 if (i & 1) ^ step else 1
        pairs.append((i, i ^ (X_LOW * hop)))
    return lax.ppermute(value, "pipe", pairs)


def dispatch(first, second):
    block = jnp.concatenate([shifted(first, 0), shifted(second, 1)], axis=0)
    two = jnp.concatenate([block, along_x(block, 0)], axis=0)
    return jnp.concatenate([two, along_x(two, 1)], axis=0)


def add(a, b):
    return (a.astype(F32) + b.astype(F32)).astype(BF)


def collect(kept, sent, after=None, last=None):
    two = add(kept, along_x(sent, 1))
    size = two.shape[0] // 2
    one = add(two[:size], along_x(two[size:], 0))
    full = add(one[:SLOT], across(one[SLOT:], Y_HI))
    chunk = shifted(full, 0)
    block = jnp.concatenate([chunk, across(chunk, Y_HI)], axis=0)
    two = block, along_x(block, 0)
    two = jnp.concatenate(two, axis=0) if after is None else join(*two, after)
    rest = along_x(two, 1)
    if last is not None:
        rest = later(rest, last)
    return two, rest, across(two, CORE), across(rest, CORE)


def dot(a, b):
    return jnp.dot(a, b, preferred_element_type=F32)


def tdot(a, b):
    return lax.dot_general(a, b, (((1,), (1,)), ((), ())), preferred_element_type=F32)


def far(value):
    return pltpu.with_memory_space_constraint(value, pltpu.HBM)


def near(value):
    return pltpu.with_memory_space_constraint(value, pltpu.VMEM)


def cost(flops, nbytes):
    return pl.CostEstimate(flops=int(flops), bytes_accessed=int(nbytes), transcendentals=0)


def tables(p, s, ids, gates, rows):
    tok = ids.shape[1]
    row = lax.broadcasted_iota(jnp.int32, (rows, tok), 0)
    far_core, k = row >> 6, (row >> 3) & 1
    ring = (row >> 4) & 3
    off = ring ^ (ring >> 1)
    off = off ^ (2 * (off & 1) * ((p & 1) ^ far_core))
    expert = s ^ delta(p, 0) ^ (far_core * 12) ^ (k * 4) ^ off
    named = jnp.zeros((rows, tok), F32)
    gate = jnp.zeros((rows, tok), F32)
    for choice in range(ids.shape[0]):
        hit = ids[choice : choice + 1, :] == expert
        named = jnp.where(hit, 1.0, named)
        gate = jnp.where(hit, gates[choice : choice + 1, :], gate)
    first = lax.broadcasted_iota(jnp.int32, (tok, tok), 0)
    second = lax.broadcasted_iota(jnp.int32, (tok, tok), 1)
    earlier = jnp.where(first < second, 1.0, 0.0).astype(BF)
    before = dot(named.astype(BF), earlier)
    slot = (row & (SLOT - 1)).astype(F32)
    here = jnp.logical_and(named > 0.5, before == slot)
    return jnp.where(here, 1.0, 0.0), jnp.where(here, gate, 0.0)


def select_kernel(
    p_ref, s_ref, ids_ref, gates_ref, tok_ref, grad_ref,
    send0, send1, dsend0, dsend1, pick, weight,
):
    @pl.when(pl.program_id(0) == 0)
    def _():
        p, s = p_ref[0], s_ref[0]
        sel, mix = tables(p, s, ids_ref[...], gates_ref[...], 2 * SLOT)
        pick[...] = sel.astype(BF)
        total = jnp.sum(mix, axis=1, keepdims=True)
        weight[...] = jnp.broadcast_to(total, weight.shape)
    rows = dot(pick[...], tok_ref[...]).astype(BF)
    drows = (dot(pick[...], grad_ref[...]) * weight[:, :1]).astype(BF)
    send0[...] = rows[:SLOT]
    send1[...] = rows[SLOT:]
    dsend0[...] = drows[:SLOT]
    dsend1[...] = drows[SLOT:]


def whole(shape):
    return pl.BlockSpec(shape, lambda i: (0,) * len(shape))


SCALAR = pl.BlockSpec(memory_space=pltpu.SMEM)


def select(p, s, ids, gates, tokens, grads):
    tok, d = tokens.shape
    wide = d // STEPS
    col = lambda rows: pl.BlockSpec((rows, wide), lambda i: (0, i))
    chunk = jax.ShapeDtypeStruct((SLOT, d), BF)
    return pl.pallas_call(
        select_kernel,
        grid=(STEPS,),
        in_specs=[
            SCALAR,
            SCALAR,
            whole(ids.shape),
            whole(gates.shape),
            col(tok),
            col(tok),
        ],
        out_specs=[col(SLOT)] * 4,
        out_shape=[chunk] * 4,
        scratch_shapes=[pltpu.VMEM((2 * SLOT, tok), BF), pltpu.VMEM((2 * SLOT, tok), F32)],
        cost_estimate=cost(4 * 2 * SLOT * tok * d, 4 * tok * d),
        compiler_params=pltpu.CompilerParams(vmem_limit_bytes=16 << 20),
        name="select",
    )(p, s, ids, gates, far(tokens), far(grads))


def latent_kernel(
    p_ref, s_ref, ids_ref, gates_ref, lat_ref, got_ref, tok_ref,
    out_ref, sel_ref, hi_ref, lo_ref, turned,
):
    i = pl.program_id(0)

    @pl.when(i == 0)
    def _():
        tok = ids_ref.shape[1]
        sel, mix = tables(p_ref[0], s_ref[0], ids_ref[...], gates_ref[...], tok)
        sel_ref[...] = sel.T.astype(BF)
        mix = mix.T
        hi = mix.astype(BF)
        hi_ref[...] = hi
        lo_ref[...] = (mix - hi.astype(F32)).astype(BF)
        width = got_ref.shape[1]
        mine = jnp.where(p_ref[0] < 8, lat_ref[0, :, :width], lat_ref[0, :, width:])
        turned[...] = (mine.astype(F32) + got_ref[...].astype(F32)).astype(BF)

    part = lax.dot_general(tok_ref[...], turned[...], (((0,), (0,)), ((), ())), preferred_element_type=F32)
    out_ref[...] = part.astype(BF)


def latent_part(p, s, ids, gates, latent, got, tokens):
    tok, d = tokens.shape
    width = got.shape[1]
    n = 16
    group = 4
    table = jax.ShapeDtypeStruct((tok, tok), BF)
    return pl.pallas_call(
        latent_kernel,
        grid=(n // group,),
        in_specs=[
            SCALAR,
            SCALAR,
            whole(ids.shape),
            whole(gates.shape),
            whole(latent.shape),
            whole(got.shape),
            pl.BlockSpec((tok, d // n * group), lambda i: (0, i)),
        ],
        out_specs=[pl.BlockSpec((d // n * group, width), lambda i: (i, 0))]
        + [whole((tok, tok))] * 3,
        out_shape=[pltpu.HBM((d, width), BF)] + [table] * 3,
        scratch_shapes=[pltpu.VMEM((tok, width), BF)],
        cost_estimate=cost(2 * tok * d * width, 2 * tok * d + 2 * d * width),
        compiler_params=pltpu.CompilerParams(vmem_limit_bytes=16 << 20),
        name="latent_part",
    )(p, s, ids, gates, latent, got, tokens)


def finish_kernel(p_ref, share_ref, theirs_ref, out_ref):
    low = p_ref[0] < 8
    share, theirs = share_ref[...], theirs_ref[...]
    width = share.shape[1]
    out_ref[0, :, :width] = jnp.where(low, share, theirs)
    out_ref[0, :, width:] = jnp.where(low, theirs, share)


def finish(p, share, theirs):
    rows, width = share.shape
    return pl.pallas_call(
        finish_kernel,
        in_specs=[SCALAR] + [pl.BlockSpec(memory_space=pltpu.VMEM)] * 2,
        out_specs=pl.BlockSpec(memory_space=pltpu.VMEM),
        out_shape=jax.ShapeDtypeStruct((1, rows, 2 * width), BF),
        cost_estimate=cost(0, 8 * width * rows),
        compiler_params=pltpu.CompilerParams(vmem_limit_bytes=8 << 20),
        name="finish",
    )(p, share, theirs)


def join_kernel(a, b, _, out):
    size = a.shape[0]
    out[:size] = a[...]
    out[size:] = b[...]


def pass_kernel(a, *refs):
    out = refs[-1]
    out[...] = a[...]


def later(a, *after):
    vmem = pl.BlockSpec(memory_space=pltpu.VMEM)
    return pl.pallas_call(
        pass_kernel,
        in_specs=[vmem] + [pl.BlockSpec(memory_space=pl.ANY)] * len(after),
        out_specs=vmem,
        out_shape=pltpu.VMEM(a.shape, a.dtype),
        cost_estimate=cost(0, 4 * a.size),
        compiler_params=pltpu.CompilerParams(vmem_limit_bytes=8 << 20),
        name="later",
    )(near(a), *after)


def join(a, b, after):
    vmem = pl.BlockSpec(memory_space=pltpu.VMEM)
    return pl.pallas_call(
        join_kernel,
        in_specs=[vmem] * 2 + [pl.BlockSpec(memory_space=pl.ANY)],
        out_specs=vmem,
        out_shape=pltpu.VMEM((2 * a.shape[0], a.shape[1]), a.dtype),
        cost_estimate=cost(0, 8 * a.size),
        compiler_params=pltpu.CompilerParams(vmem_limit_bytes=8 << 20),
        name="join",
    )(near(a), near(b), after)


PIECES = 7


def forward_kernel(rows, wg, wu, wg2, wu2, wd, wd2, _, kept, sent, fa, fb):
    n, d = rows.shape
    f = wg.shape[1]
    wide = d // PIECES
    acc = jnp.zeros((n, 4 * f), F32)
    for i in range(PIECES):
        at = pl.ds(i * wide, wide)
        weights = jnp.concatenate([wg[at, :], wg2[at, :], wu[at, :], wu2[at, :]], axis=1)
        acc = acc + dot(rows[:, at], weights)
    gate, up = acc[:, : 2 * f], acc[:, 2 * f :]
    sg = jax.nn.sigmoid(gate)
    hidden = (gate * sg * up).astype(BF)
    fa[...] = up * sg * (1.0 + gate * (1.0 - sg))
    fb[...] = gate * sg
    for i in range(PIECES):
        at = pl.ds(i * wide, wide)
        out = dot(hidden, jnp.concatenate([wd[:, at], wd2[:, at]], axis=0)).astype(BF)
        kept[:, at] = out[: n // 2]
        sent[:, at] = out[n // 2 :]


def forward(rows, wg, wu, wg2, wu2, wd, wd2, after):
    n, d = rows.shape
    f = wg.shape[1]
    vmem = pl.BlockSpec(memory_space=pltpu.VMEM)
    return pl.pallas_call(
        forward_kernel,
        in_specs=[vmem] * 7 + [pl.BlockSpec(memory_space=pl.ANY)],
        out_specs=[vmem] * 4,
        out_shape=[pltpu.VMEM((n // 2, d), BF)] * 2 + [pltpu.VMEM((n, 2 * f), F32)] * 2,
        cost_estimate=cost(12 * n * d * f, 12 * d * f + 4 * n * d),
        compiler_params=pltpu.CompilerParams(vmem_limit_bytes=12 << 20),
        name="forward",
    )(*map(near, (rows, wg, wu, wg2, wu2, wd, wd2)), after)


def backward_kernel(rows, fa, fb, wd, wd2, wg, wu, wg2, wu2, kept, sent):
    n, d = rows.shape
    f = wg.shape[1]
    wide = d // PIECES
    acc = jnp.zeros((n, 2 * f), F32)
    for i in range(PIECES):
        at = pl.ds(i * wide, wide)
        acc = acc + tdot(rows[:, at], jnp.concatenate([wd[:, at], wd2[:, at]], axis=0))
    grads = jnp.concatenate([(acc * fa[...]).astype(BF), (acc * fb[...]).astype(BF)], axis=1)
    for i in range(PIECES):
        at = pl.ds(i * wide, wide)
        weights = jnp.concatenate([wg[at, :], wg2[at, :], wu[at, :], wu2[at, :]], axis=1)
        out = tdot(grads, weights).astype(BF)
        kept[:, at] = out[: n // 2]
        sent[:, at] = out[n // 2 :]


def backward(rows, fa, fb, wd, wd2, wg, wu, wg2, wu2):
    n, d = rows.shape
    f = wg.shape[1]
    vmem = pl.BlockSpec(memory_space=pltpu.VMEM)
    return pl.pallas_call(
        backward_kernel,
        in_specs=[vmem] * 9,
        out_specs=[vmem] * 2,
        out_shape=[pltpu.VMEM((n // 2, d), BF)] * 2,
        cost_estimate=cost(12 * n * d * f, 12 * d * f + 4 * n * d),
        compiler_params=pltpu.CompilerParams(vmem_limit_bytes=12 << 20),
        name="backward",
    )(*map(near, (rows, fa, fb, wd, wd2, wg, wu, wg2, wu2)))


def combine_kernel(n_tables, *refs):
    mixing, parts, out, buf, sems = refs[:n_tables], refs[n_tables:-3], *refs[-3:]
    d = out.shape[1]
    wide = d // PIECES
    copies = []
    for i in range(PIECES):
        at = pl.ds(i * wide, wide)
        back = jnp.concatenate([part[:, at] for part in parts], axis=0)
        total = dot(mixing[0][...], back)
        for table in mixing[1:]:
            total = total + dot(table[...], back)
        buf[:, at] = total.astype(BF)
        copy = pltpu.make_async_copy(buf.at[:, at], out.at[:, at], sems.at[i])
        copy.start()
        copies.append(copy)
    for copy in copies:
        copy.wait()


def combine(mixing, parts):
    tok = mixing[0].shape[0]
    d = parts[0].shape[1]
    vmem = pl.BlockSpec(memory_space=pltpu.VMEM)
    return pl.pallas_call(
        functools.partial(combine_kernel, len(mixing)),
        in_specs=[vmem] * (len(mixing) + len(parts)),
        out_specs=pl.BlockSpec(memory_space=pl.ANY),
        out_shape=jax.ShapeDtypeStruct((tok, d), BF),
        scratch_shapes=[pltpu.VMEM((tok, d), BF), pltpu.SemaphoreType.DMA((PIECES,))],
        cost_estimate=cost(2 * tok * tok * d * len(mixing), 4 * tok * d),
        compiler_params=pltpu.CompilerParams(vmem_limit_bytes=12 << 20),
        name="combine",
    )(*map(near, mixing), *map(near, parts))


def per_device(tokens, route_ids, route_gates, w_gate, w_up, w_down, out_grad, latent_grad):
    p = lax.axis_index("pipe").reshape(1).astype(jnp.int32)
    s = lax.axis_index("expert").reshape(1).astype(jnp.int32)
    ids, gates = route_ids.T, route_gates.T
    wg, wu, wd = w_gate[0], w_up[0], w_down[0]
    wg2, wu2, wd2 = across(wg, CORE), across(wu, CORE), across(wd, CORE)
    mirror = [(i, 15 - i) for i in range(16)]

    send0, send1, dsend0, dsend1 = select(p, s, ids, gates, tokens, out_grad)
    latent = latent_grad[0]
    width = latent.shape[1] // 2
    other = jnp.where(p[0] < 8, latent[:, width:], latent[:, :width])
    got = lax.ppermute(other, "pipe", mirror)
    send0 = later(send0, got, wg2)
    part, sel, hi, lo = latent_part(p, s, ids, gates, latent_grad, got, tokens)
    share = lax.psum_scatter(part, "expert", scatter_dimension=0, tiled=True)
    theirs = lax.ppermute(share, "pipe", mirror)
    kv_grad = finish(p, share, theirs)

    rows = dispatch(send0, send1)
    drows = dispatch(dsend0, dsend1)
    kept, sent, fa, fb = forward(rows, wg, wu, wg2, wu2, wd, wd2, hi)
    routed = combine([hi, lo], collect(kept, sent))
    dkept, dsent = backward(drows, fa, fb, wd, wd2, wg, wu, wg2, wu2)
    token_grad = combine([sel], collect(dkept, dsent, sel, theirs))
    return routed, token_grad, kv_grad


def solution(mesh):
    return jax.shard_map(
        per_device,
        mesh=mesh,
        in_specs=(
            P("expert", None),
            P("expert", None),
            P("expert", None),
            P("expert", None, "pipe"),
            P("expert", None, "pipe"),
            P("expert", "pipe", None),
            P("expert", None),
            P("pipe", "expert", None),
        ),
        out_specs=(P("expert", None), P("expert", None), P("pipe", "expert", None)),
        check_vma=False,
    )
```

```python
import functools
import jax
import jax.numpy as jnp
from jax import lax
from jax.experimental import pallas as pl
from jax.experimental.pallas import tpu as pltpu
from jax.sharding import PartitionSpec as P

SLOT = 8
BF = jnp.bfloat16
F32 = jnp.float32
CORE, Y_HI, X_LOW = 1, 2, 4
STEPS = 4


def across(value, mask):
    return lax.ppermute(value, "pipe", [(i, i ^ mask) for i in range(16)])


def delta(p, k):
    return (p & 1) * 8 + (k ^ ((p ^ (p >> 1)) & 1)) * 4 + (p >> 2)


def shifted(value, k):
    pairs = [(p * 16 + e, p * 16 + (e ^ delta(p, k))) for p in range(16) for e in range(16)]
    return lax.ppermute(value, ("pipe", "expert"), pairs)


def along_x(value, step):
    pairs = []
    for i in range(16):
        hop = 3 if (i & 1) ^ step else 1
        pairs.append((i, i ^ (X_LOW * hop)))
    return lax.ppermute(value, "pipe", pairs)


def dispatch(first, second):
    block = jnp.concatenate([shifted(first, 0), shifted(second, 1)], axis=0)
    two = jnp.concatenate([block, along_x(block, 0)], axis=0)
    return jnp.concatenate([two, along_x(two, 1)], axis=0)


def add(a, b):
    return (a.astype(F32) + b.astype(F32)).astype(BF)


def collect(kept, sent, after=None, last=None):
    two = add(kept, along_x(sent, 1))
    size = two.shape[0] // 2
    one = add(two[:size], along_x(two[size:], 0))
    full = add(one[:SLOT], across(one[SLOT:], Y_HI))
    chunk = shifted(full, 0)
    block = jnp.concatenate([chunk, across(chunk, Y_HI)], axis=0)
    two = block, along_x(block, 0)
    two = jnp.concatenate(two, axis=0) if after is None else join(*two, after)
    rest = along_x(two, 1)
    if last is not None:
        rest = later(rest, last)
    return two, rest, across(two, CORE), across(rest, CORE)


def dot(a, b):
    return jnp.dot(a, b, preferred_element_type=F32)


def tdot(a, b):
    return lax.dot_general(a, b, (((1,), (1,)), ((), ())), preferred_element_type=F32)


def far(value):
    return pltpu.with_memory_space_constraint(value, pltpu.HBM)


def near(value):
    return pltpu.with_memory_space_constraint(value, pltpu.VMEM)


def cost(flops, nbytes):
    return pl.CostEstimate(flops=int(flops), bytes_accessed=int(nbytes), transcendentals=0)


def tables(p, s, ids, gates, rows):
    tok = ids.shape[1]
    row = lax.broadcasted_iota(jnp.int32, (rows, tok), 0)
    far_core, k = row >> 6, (row >> 3) & 1
    ring = (row >> 4) & 3
    off = ring ^ (ring >> 1)
    off = off ^ (2 * (off & 1) * ((p & 1) ^ far_core))
    expert = s ^ delta(p, 0) ^ (far_core * 12) ^ (k * 4) ^ off
    named = jnp.zeros((rows, tok), F32)
    gate = jnp.zeros((rows, tok), F32)
    for choice in range(ids.shape[0]):
        hit = ids[choice : choice + 1, :] == expert
        named = jnp.where(hit, 1.0, named)
        gate = jnp.where(hit, gates[choice : choice + 1, :], gate)
    first = lax.broadcasted_iota(jnp.int32, (tok, tok), 0)
    second = lax.broadcasted_iota(jnp.int32, (tok, tok), 1)
    earlier = jnp.where(first < second, 1.0, 0.0).astype(BF)
    before = dot(named.astype(BF), earlier)
    slot = (row & (SLOT - 1)).astype(F32)
    here = jnp.logical_and(named > 0.5, before == slot)
    return jnp.where(here, 1.0, 0.0), jnp.where(here, gate, 0.0)


def select_kernel(
    p_ref, s_ref, ids_ref, gates_ref, tok_ref, grad_ref,
    send0, send1, dsend0, dsend1, pick, weight,
):
    @pl.when(pl.program_id(0) == 0)
    def _():
        p, s = p_ref[0], s_ref[0]
        sel, mix = tables(p, s, ids_ref[...], gates_ref[...], 2 * SLOT)
        pick[...] = sel.astype(BF)
        total = jnp.sum(mix, axis=1, keepdims=True)
        weight[...] = jnp.broadcast_to(total, weight.shape)
    rows = dot(pick[...], tok_ref[...]).astype(BF)
    drows = (dot(pick[...], grad_ref[...]) * weight[:, :1]).astype(BF)
    send0[...] = rows[:SLOT]
    send1[...] = rows[SLOT:]
    dsend0[...] = drows[:SLOT]
    dsend1[...] = drows[SLOT:]


def whole(shape):
    return pl.BlockSpec(shape, lambda i: (0,) * len(shape))


SCALAR = pl.BlockSpec(memory_space=pltpu.SMEM)


def select(p, s, ids, gates, tokens, grads):
    tok, d = tokens.shape
    wide = d // STEPS
    col = lambda rows: pl.BlockSpec((rows, wide), lambda i: (0, i))
    chunk = jax.ShapeDtypeStruct((SLOT, d), BF)
    return pl.pallas_call(
        select_kernel,
        grid=(STEPS,),
        in_specs=[
            SCALAR,
            SCALAR,
            whole(ids.shape),
            whole(gates.shape),
            col(tok),
            col(tok),
        ],
        out_specs=[col(SLOT)] * 4,
        out_shape=[chunk] * 4,
        scratch_shapes=[pltpu.VMEM((2 * SLOT, tok), BF), pltpu.VMEM((2 * SLOT, tok), F32)],
        cost_estimate=cost(4 * 2 * SLOT * tok * d, 4 * tok * d),
        compiler_params=pltpu.CompilerParams(vmem_limit_bytes=16 << 20),
        name="select",
    )(p, s, ids, gates, far(tokens), far(grads))


def latent_kernel(
    p_ref, s_ref, ids_ref, gates_ref, lat_ref, got_ref, tok_ref,
    out_ref, sel_ref, hi_ref, lo_ref, turned,
):
    i = pl.program_id(0)

    @pl.when(i == 0)
    def _():
        tok = ids_ref.shape[1]
        sel, mix = tables(p_ref[0], s_ref[0], ids_ref[...], gates_ref[...], tok)
        sel_ref[...] = sel.T.astype(BF)
        mix = mix.T
        hi = mix.astype(BF)
        hi_ref[...] = hi
        lo_ref[...] = (mix - hi.astype(F32)).astype(BF)
        width = got_ref.shape[1]
        mine = jnp.where(p_ref[0] < 8, lat_ref[0, :, :width], lat_ref[0, :, width:])
        turned[...] = (mine.astype(F32) + got_ref[...].astype(F32)).astype(BF)

    part = lax.dot_general(tok_ref[...], turned[...], (((0,), (0,)), ((), ())), preferred_element_type=F32)
    out_ref[...] = part.astype(BF)


def latent_part(p, s, ids, gates, latent, got, tokens):
    tok, d = tokens.shape
    width = got.shape[1]
    n = 16
    group = 2
    table = jax.ShapeDtypeStruct((tok, tok), BF)
    return pl.pallas_call(
        latent_kernel,
        grid=(n // group,),
        in_specs=[
            SCALAR,
            SCALAR,
            whole(ids.shape),
            whole(gates.shape),
            whole(latent.shape),
            whole(got.shape),
            pl.BlockSpec((tok, d // n * group), lambda i: (0, i)),
        ],
        out_specs=[pl.BlockSpec((d // n * group, width), lambda i: (i, 0))]
        + [whole((tok, tok))] * 3,
        out_shape=[pltpu.HBM((d, width), BF)] + [table] * 3,
        scratch_shapes=[pltpu.VMEM((tok, width), BF)],
        cost_estimate=cost(2 * tok * d * width, 2 * tok * d + 2 * d * width),
        compiler_params=pltpu.CompilerParams(vmem_limit_bytes=16 << 20),
        name="latent_part",
    )(p, s, ids, gates, latent, got, near(tokens))


def finish_kernel(p_ref, share_ref, theirs_ref, out_ref):
    low = p_ref[0] < 8
    share, theirs = share_ref[...], theirs_ref[...]
    width = share.shape[1]
    out_ref[0, :, :width] = jnp.where(low, share, theirs)
    out_ref[0, :, width:] = jnp.where(low, theirs, share)


def finish(p, share, theirs):
    rows, width = share.shape
    return pl.pallas_call(
        finish_kernel,
        in_specs=[SCALAR] + [pl.BlockSpec(memory_space=pltpu.VMEM)] * 2,
        out_specs=pl.BlockSpec(memory_space=pltpu.VMEM),
        out_shape=jax.ShapeDtypeStruct((1, rows, 2 * width), BF),
        cost_estimate=cost(0, 8 * width * rows),
        compiler_params=pltpu.CompilerParams(vmem_limit_bytes=8 << 20),
        name="finish",
    )(p, share, theirs)


def join_kernel(a, b, _, out):
    size = a.shape[0]
    out[:size] = a[...]
    out[size:] = b[...]


def pass_kernel(a, *refs):
    out = refs[-1]
    out[...] = a[...]


def later(a, *after):
    vmem = pl.BlockSpec(memory_space=pltpu.VMEM)
    return pl.pallas_call(
        pass_kernel,
        in_specs=[vmem] + [pl.BlockSpec(memory_space=pl.ANY)] * len(after),
        out_specs=vmem,
        out_shape=pltpu.VMEM(a.shape, a.dtype),
        cost_estimate=cost(0, 4 * a.size),
        compiler_params=pltpu.CompilerParams(vmem_limit_bytes=8 << 20),
        name="later",
    )(near(a), *after)


def join(a, b, after):
    vmem = pl.BlockSpec(memory_space=pltpu.VMEM)
    return pl.pallas_call(
        join_kernel,
        in_specs=[vmem] * 2 + [pl.BlockSpec(memory_space=pl.ANY)],
        out_specs=vmem,
        out_shape=pltpu.VMEM((2 * a.shape[0], a.shape[1]), a.dtype),
        cost_estimate=cost(0, 8 * a.size),
        compiler_params=pltpu.CompilerParams(vmem_limit_bytes=8 << 20),
        name="join",
    )(near(a), near(b), after)


PIECES = 7


def forward_kernel(rows, wg, wu, wg2, wu2, wd, wd2, _, kept, sent, fa, fb):
    n, d = rows.shape
    f = wg.shape[1]
    wide = d // PIECES
    acc = jnp.zeros((n, 4 * f), F32)
    for i in range(PIECES):
        at = pl.ds(i * wide, wide)
        weights = jnp.concatenate([wg[at, :], wg2[at, :], wu[at, :], wu2[at, :]], axis=1)
        acc = acc + dot(rows[:, at], weights)
    gate, up = acc[:, : 2 * f], acc[:, 2 * f :]
    sg = jax.nn.sigmoid(gate)
    hidden = (gate * sg * up).astype(BF)
    fa[...] = up * sg * (1.0 + gate * (1.0 - sg))
    fb[...] = gate * sg
    for i in range(PIECES):
        at = pl.ds(i * wide, wide)
        out = dot(hidden, jnp.concatenate([wd[:, at], wd2[:, at]], axis=0)).astype(BF)
        kept[:, at] = out[: n // 2]
        sent[:, at] = out[n // 2 :]


def forward(rows, wg, wu, wg2, wu2, wd, wd2, after):
    n, d = rows.shape
    f = wg.shape[1]
    vmem = pl.BlockSpec(memory_space=pltpu.VMEM)
    return pl.pallas_call(
        forward_kernel,
        in_specs=[vmem] * 7 + [pl.BlockSpec(memory_space=pl.ANY)],
        out_specs=[vmem] * 4,
        out_shape=[pltpu.VMEM((n // 2, d), BF)] * 2 + [pltpu.VMEM((n, 2 * f), F32)] * 2,
        cost_estimate=cost(12 * n * d * f, 12 * d * f + 4 * n * d),
        compiler_params=pltpu.CompilerParams(vmem_limit_bytes=12 << 20),
        name="forward",
    )(*map(near, (rows, wg, wu, wg2, wu2, wd, wd2)), after)


def backward_kernel(rows, fa, fb, wd, wd2, wg, wu, wg2, wu2, kept, sent):
    n, d = rows.shape
    f = wg.shape[1]
    wide = d // PIECES
    acc = jnp.zeros((n, 2 * f), F32)
    for i in range(PIECES):
        at = pl.ds(i * wide, wide)
        acc = acc + tdot(rows[:, at], jnp.concatenate([wd[:, at], wd2[:, at]], axis=0))
    grads = jnp.concatenate([(acc * fa[...]).astype(BF), (acc * fb[...]).astype(BF)], axis=1)
    for i in range(PIECES):
        at = pl.ds(i * wide, wide)
        weights = jnp.concatenate([wg[at, :], wg2[at, :], wu[at, :], wu2[at, :]], axis=1)
        out = tdot(grads, weights).astype(BF)
        kept[:, at] = out[: n // 2]
        sent[:, at] = out[n // 2 :]


def backward(rows, fa, fb, wd, wd2, wg, wu, wg2, wu2):
    n, d = rows.shape
    f = wg.shape[1]
    vmem = pl.BlockSpec(memory_space=pltpu.VMEM)
    return pl.pallas_call(
        backward_kernel,
        in_specs=[vmem] * 9,
        out_specs=[vmem] * 2,
        out_shape=[pltpu.VMEM((n // 2, d), BF)] * 2,
        cost_estimate=cost(12 * n * d * f, 12 * d * f + 4 * n * d),
        compiler_params=pltpu.CompilerParams(vmem_limit_bytes=12 << 20),
        name="backward",
    )(*map(near, (rows, fa, fb, wd, wd2, wg, wu, wg2, wu2)))


def combine_kernel(n_tables, *refs):
    mixing, parts, out, buf, sems = refs[:n_tables], refs[n_tables:-3], *refs[-3:]
    d = out.shape[1]
    wide = d // PIECES
    copies = []
    for i in range(PIECES):
        at = pl.ds(i * wide, wide)
        back = jnp.concatenate([part[:, at] for part in parts], axis=0)
        total = dot(mixing[0][...], back)
        for table in mixing[1:]:
            total = total + dot(table[...], back)
        buf[:, at] = total.astype(BF)
        copy = pltpu.make_async_copy(buf.at[:, at], out.at[:, at], sems.at[i])
        copy.start()
        copies.append(copy)
    for copy in copies:
        copy.wait()


def combine(mixing, parts):
    tok = mixing[0].shape[0]
    d = parts[0].shape[1]
    vmem = pl.BlockSpec(memory_space=pltpu.VMEM)
    return pl.pallas_call(
        functools.partial(combine_kernel, len(mixing)),
        in_specs=[vmem] * (len(mixing) + len(parts)),
        out_specs=pl.BlockSpec(memory_space=pl.ANY),
        out_shape=jax.ShapeDtypeStruct((tok, d), BF),
        scratch_shapes=[pltpu.VMEM((tok, d), BF), pltpu.SemaphoreType.DMA((PIECES,))],
        cost_estimate=cost(2 * tok * tok * d * len(mixing), 4 * tok * d),
        compiler_params=pltpu.CompilerParams(vmem_limit_bytes=12 << 20),
        name="combine",
    )(*map(near, mixing), *map(near, parts))


def per_device(tokens, route_ids, route_gates, w_gate, w_up, w_down, out_grad, latent_grad):
    p = lax.axis_index("pipe").reshape(1).astype(jnp.int32)
    s = lax.axis_index("expert").reshape(1).astype(jnp.int32)
    ids, gates = route_ids.T, route_gates.T
    wg, wu, wd = w_gate[0], w_up[0], w_down[0]
    wg2, wu2, wd2 = across(wg, CORE), across(wu, CORE), across(wd, CORE)
    mirror = [(i, 15 - i) for i in range(16)]

    send0, send1, dsend0, dsend1 = select(p, s, ids, gates, tokens, out_grad)
    latent = latent_grad[0]
    width = latent.shape[1] // 2
    other = jnp.where(p[0] < 8, latent[:, width:], latent[:, :width])
    got = lax.ppermute(other, "pipe", mirror)
    send0 = later(send0, got, wg2)
    part, sel, hi, lo = latent_part(p, s, ids, gates, latent_grad, got, tokens)
    share = lax.psum_scatter(part, "expert", scatter_dimension=0, tiled=True)
    theirs = lax.ppermute(share, "pipe", mirror)
    kv_grad = finish(p, share, theirs)

    rows = dispatch(send0, send1)
    drows = dispatch(dsend0, dsend1)
    kept, sent, fa, fb = forward(rows, wg, wu, wg2, wu2, wd, wd2, hi)
    routed = combine([hi, lo], collect(kept, sent))
    dkept, dsent = backward(drows, fa, fb, wd, wd2, wg, wu, wg2, wu2)
    token_grad = combine([sel], collect(dkept, dsent, sel, theirs))
    return routed, token_grad, kv_grad


def solution(mesh):
    return jax.shard_map(
        per_device,
        mesh=mesh,
        in_specs=(
            P("expert", None),
            P("expert", None),
            P("expert", None),
            P("expert", None, "pipe"),
            P("expert", None, "pipe"),
            P("expert", "pipe", None),
            P("expert", None),
            P("pipe", "expert", None),
        ),
        out_specs=(P("expert", None), P("expert", None), P("pipe", "expert", None)),
        check_vma=False,
    )
```
